32 devices in a mesh: row: 8 (over z, x), rep: 4 (over y, core).
Axes of the slice: x: 2, y: 2, z: 4, core: 2. Of those that a mesh axis runs over, the one named last changes fastest.
Arguments:
- features: bfloat16 [8192, 256], P('row'), may hold values from -6 to 6
- block_cols: int32 [64, 4, 12], P('row', 'rep'), may hold values from 0 to 63, as said below
- block_vals: bfloat16 [64, 4, 12, 128, 128], P('row', 'rep'), may hold values from -0.078125 to 0.078125
- weight: bfloat16 [256, 256], replicated, may hold values from -0.375 to 0.375
- cotangent: bfloat16 [8192, 256], P(('row', 'rep')), may hold values from -6 to 6
Outputs:
- output_rows: bfloat16 [8192, 256], P(('row', 'rep'))
- grad_weight: float32 [256, 256], replicated
- grad_features: float32 [8192, 256], P(('row', 'rep'))
The draws below stay inside these ranges and needn't reach their ends.
Inputs may be any that keep to these rules, and one draw needn't show every extreme that they name: For a node block b of row group g = b // 8 and quarter index r, every entry block_cols[b, r, s] equals h * 8 + r * 2 + q with h a row group within 3 of g (and inside the grid) and 0 <= q < 2; entries may repeat.
All inputs are finite; a program needn't handle non-finite values.
Results may differ from the reference program's by a relative error of at most 0.0065.
Values may be sent and summed in bfloat16 or wider, within the bound.
A program may use at most 64 MiB of HBM per device.

```python
import jax
import jax.numpy as jnp
from jax import lax

HID = 256
BLK = 128
BR = 8
HALF = 3
SLOTS = 12
QUART = 2
ROWBLOCKS = 64
NODES = 8192
N_ROW = 8
N_REP = 4


def draw_block_cols(key, part):
    groups = jnp.arange(ROWBLOCKS) // BR
    lowest = jnp.maximum(groups - HALF, 0)
    highest = jnp.minimum(groups + HALF, N_ROW - 1)
    first_key, second_key = jax.random.split(key)
    dims = (ROWBLOCKS, N_REP, SLOTS)
    source = jax.random.randint(first_key, dims, lowest[:, None, None], highest[:, None, None] + 1)
    within = jax.random.randint(second_key, dims, 0, QUART)
    replica_base = jnp.arange(N_REP)[None, :, None] * QUART
    return (source * BR + replica_base + within).astype(jnp.int32)


def level_of(stream_key, extent, cuts, smallest, top_value):
    def one(position, shards_of):
        steps = jax.random.uniform(jax.random.fold_in(jax.random.fold_in(stream_key, 6), position), (shards_of,), jnp.float32, smallest / len(cuts), top_value / len(cuts))
        return jnp.repeat(jnp.exp(steps), extent[position] // shards_of).reshape((-1,) + (1,) * (len(extent) - position - 1))

    factor_of = one(*cuts[0])
    for cut in cuts[1:]:
        factor_of = factor_of * one(*cut)
    return factor_of


def scatter_about(stream_key, shape, deviation, reach, cuts=(), held_as=jnp.bfloat16):
    entries = deviation * jax.random.normal(stream_key, shape, jnp.float32)
    if cuts:
        entries = entries * level_of(stream_key, shape, cuts, -0.22, 0.18)
    return jnp.clip(entries, -reach, reach).astype(held_as)


def setup_inputs(seed: int = 0) -> dict:
    seeds = jax.random.split(jax.random.key(seed), 6)
    features = scatter_about(seeds[0], (NODES, HID), 1.0, 6.0, ((0, 8),))
    block_cols = draw_block_cols(jax.random.fold_in(seeds[5], 71), 0)
    block_vals = scatter_about(seeds[2], (ROWBLOCKS, N_REP, SLOTS, BLK, BLK), (N_REP * SLOTS * BLK) ** -0.5, 0.078125, ((0, 8), (1, 4)))
    weight = scatter_about(seeds[3], (HID, HID), HID ** -0.5, 0.375)
    cotangent = scatter_about(seeds[4], (NODES, HID), 1.0, 6.0, ((0, 32),))
    return {"features": features, "block_cols": block_cols, "block_vals": block_vals, "weight": weight, "cotangent": cotangent}


def reference(features, block_cols, block_vals, weight, cotangent):
    feature_blocks = features.reshape(ROWBLOCKS, BLK, HID)
    column_ids = block_cols.reshape(ROWBLOCKS, N_REP * SLOTS)
    block_values = block_vals.reshape(ROWBLOCKS, N_REP * SLOTS, BLK, BLK)

    def row_block(payload):
        columns, values = payload
        picked = feature_blocks[columns].astype(jnp.float32)
        return jnp.einsum("sij,sjh->ih", values.astype(jnp.float32), picked)

    aggregate = lax.map(row_block, (column_ids, block_values)).reshape(NODES, HID).astype(jnp.bfloat16)
    preact = jnp.dot(aggregate, weight, preferred_element_type=jnp.float32)
    output_rows = jax.nn.silu(preact).astype(jnp.bfloat16)
    sigmoid_pre = jax.nn.sigmoid(preact)
    grad_pre = (cotangent.astype(jnp.float32) * sigmoid_pre * (1.0 + preact * (1.0 - sigmoid_pre))).astype(jnp.bfloat16)
    grad_weight = jnp.dot(aggregate.T, grad_pre, preferred_element_type=jnp.float32) * (NODES ** -0.5)
    back_rows = jnp.dot(grad_pre, weight.T, preferred_element_type=jnp.float32).astype(jnp.bfloat16)
    back_blocks = back_rows.reshape(ROWBLOCKS, BLK, HID)

    def accumulate(accumulated, payload):
        columns, values, backward = payload
        contribution = jnp.einsum("sji,jh->sih", values.astype(jnp.float32), backward.astype(jnp.float32))
        return accumulated.at[columns].add(contribution), None

    zero_blocks = jnp.zeros((ROWBLOCKS, BLK, HID), jnp.float32)
    grad_blocks, unused = lax.scan(accumulate, zero_blocks, (column_ids, block_values, back_blocks))
    return output_rows, grad_weight, grad_blocks.reshape(NODES, HID)
```

```python
import functools

import jax
import jax.numpy as jnp
from jax import lax
from jax.experimental import pallas as pl
from jax.experimental.pallas import tpu as pltpu
from jax.sharding import PartitionSpec as P

HALF = 3
SECTIONS = 2 * HALF + 1


def flip(index, bit):
    return index + bit * (1 - 2 * ((index // bit) % 2))


def flip_all(index, mask):
    bit = 1
    while bit <= mask:
        if mask & bit:
            index = flip(index, bit)
        bit *= 2
    return index


def remote(src, dst, send_sem, recv_sem, device):
    return pltpu.make_async_remote_copy(
        src_ref=src,
        dst_ref=dst,
        send_sem=send_sem,
        recv_sem=recv_sem,
        device_id=device,
        device_id_type=pl.DeviceIdType.MESH,
    )


def layer_kernel(
    sizes,
    plan_ref, features_ref, vals_ref, weight_ref, cotangent_ref,
    out_ref, grad_weight_ref, grad_features_ref,
    vals, window, part_send, part_recv, back, run, back_send, back_recv,
    gw_send, gw_recv, bf_send, bf_recv, gw_all,
    local_sem, a_send, a_recv, b_send, b_recv, c_send, c_recv,
    d_send, d_recv, e_send, e_recv, f_send, f_recv, g_send, g_recv,
):
    rows, reps, quart, slots, blk, blocks = sizes
    pairs = blocks * slots
    row = lax.axis_index("row")
    rep = lax.axis_index("rep")
    bits = [1 << k for k in range(rows.bit_length() - 1)]
    offsets = [d for d in (3, -3, 2, -2, 1, -1)]
    masks = sorted(range(1, reps), key=lambda m: -m)

    def inside(d):
        return jnp.logical_and(row + d >= 0, row + d < rows)

    vals_copy = pltpu.make_async_copy(vals_ref, vals, local_sem.at[0])
    vals_copy.start()
    own = features_ref.at[pl.ds(rep * quart, quart)]
    own_copy = pltpu.make_async_copy(own, window.at[pl.ds(HALF * quart, quart)], local_sem.at[1])
    own_copy.start()

    barrier = pltpu.get_barrier_semaphore()
    expected = reps - 1
    for d in offsets:
        @pl.when(inside(d))
        def _():
            pl.semaphore_signal(
                barrier, inc=1, device_id=(row + d, rep), device_id_type=pl.DeviceIdType.MESH
            )
        expected = expected + inside(d).astype(jnp.int32)
    for bit in bits:
        if bit > 2:
            pl.semaphore_signal(
                barrier, inc=1, device_id=(flip(row, bit), rep),
                device_id_type=pl.DeviceIdType.MESH,
            )
            expected = expected + 1
    for mask in masks:
        pl.semaphore_signal(
            barrier, inc=1, device_id=(row, flip_all(rep, mask)),
            device_id_type=pl.DeviceIdType.MESH,
        )
    pl.semaphore_wait(barrier, expected)

    def section(ref, j):
        return ref.at[pl.ds(j * quart, quart)]

    def feature_copy(d):
        return remote(
            own, section(window, HALF - d), a_send.at[HALF - d], a_recv.at[HALF - d],
            (row + d, rep),
        )

    for d in offsets:
        @pl.when(inside(d))
        def _():
            feature_copy(d).start()

        @pl.when(jnp.logical_not(inside(d)))
        def _():
            for q in range(quart):
                window[(HALF + d) * quart + q] = jnp.zeros(window.shape[1:], window.dtype)
                back_recv[(HALF + d) * quart + q] = jnp.zeros(
                    back_recv.shape[1:], back_recv.dtype
                )
    vals_copy.wait()
    own_copy.wait()
    for d in offsets:
        @pl.when(inside(d))
        def _():
            remote(
                own, section(window, HALF + d), a_send.at[HALF + d], a_recv.at[HALF + d],
                (row + d, rep),
            ).wait_recv()

    def partial(b):
        total = None
        for s in range(0, slots, 2):
            left = jnp.concatenate([vals[b * slots + s], vals[b * slots + s + 1]], axis=1)
            right = jnp.concatenate(
                [window[plan_ref[b * slots + s]], window[plan_ref[b * slots + s + 1]]], axis=0
            )
            term = jnp.dot(left, right, preferred_element_type=jnp.float32)
            total = term if total is None else total + term
        return total

    def part_copy(mask):
        return remote(
            part_send.at[mask - 1], part_recv.at[mask - 1], b_send.at[mask - 1],
            b_recv.at[mask - 1], (row, flip_all(rep, mask)),
        )

    for mask in masks:
        target = flip_all(rep, mask)
        for q in range(quart):
            part_send[mask - 1, q * blk:(q + 1) * blk] = partial(target * quart + q).astype(
                jnp.bfloat16
            )
        part_copy(mask).start()
    total = jnp.concatenate([partial(rep * quart + q) for q in range(quart)], axis=0)
    for mask in reversed(masks):
        part_copy(mask).wait_recv()
        total = total + part_recv[mask - 1].astype(jnp.float32)

    aggregate = total.astype(jnp.bfloat16)
    weight = weight_ref[...]
    preact = jnp.dot(aggregate, weight, preferred_element_type=jnp.float32)
    sigmoid_pre = jax.nn.sigmoid(preact)
    grad_pre = (
        cotangent_ref[...].astype(jnp.float32)
        * sigmoid_pre
        * (1.0 + preact * (1.0 - sigmoid_pre))
    ).astype(jnp.bfloat16)
    back_t = lax.dot_general(
        weight, grad_pre, (((1,), (1,)), ((), ())), preferred_element_type=jnp.float32
    ).astype(jnp.bfloat16)
    for q in range(quart):
        back[rep * quart + q] = back_t[:, q * blk:(q + 1) * blk]

    def back_copy(mask, owner):
        spot = section(back, owner)
        return remote(
            spot, spot, c_send.at[mask - 1], c_recv.at[mask - 1], (row, flip_all(rep, mask))
        )

    for mask in masks:
        back_copy(mask, rep).start()
    out_ref[...] = (preact * sigmoid_pre).astype(jnp.bfloat16)

    gw_send[...] = lax.dot_general(
        aggregate, grad_pre, (((0,), (0,)), ((), ())), preferred_element_type=jnp.float32
    )
    share = gw_send.shape[0] // reps

    def share_of(ref, owner):
        return ref.at[pl.ds(owner * share, share)]

    def scatter_copy(mask):
        target = flip_all(rep, mask)
        return remote(
            share_of(gw_send, target), gw_recv.at[mask - 1], e_send.at[mask - 1],
            e_recv.at[mask - 1], (row, target),
        )

    def row_copy(k):
        return remote(
            bf_send.at[k], bf_recv.at[k], f_send.at[k], f_recv.at[k], (flip(row, bits[k]), rep)
        )

    def gather_copy(mask, owner):
        spot = share_of(gw_all, owner)
        return remote(
            spot, spot, g_send.at[mask - 1], g_recv.at[mask - 1], (row, flip_all(rep, mask))
        )

    for mask in masks:
        scatter_copy(mask).start()
    for mask in reversed(masks):
        back_copy(mask, flip_all(rep, mask)).wait_recv()

    def backward(start, stop, acc):
        def step(k, acc):
            pair = plan_ref[pairs + k]
            block = plan_ref[2 * pairs + k]
            keep = plan_ref[3 * pairs + k]
            term = jnp.dot(back[block], vals[pair], preferred_element_type=jnp.float32)
            acc = jnp.where(keep > 0, acc, 0.0) + term
            run[k] = acc
            return acc
        return lax.fori_loop(start, stop, step, acc, unroll=8)

    acc = jnp.zeros(run.shape[1:], jnp.float32)
    acc = backward(0, pairs // 3, acc)
    mine = gw_send[pl.ds(rep * share, share)]
    for mask in reversed(masks):
        scatter_copy(mask).wait_recv()
        mine = mine + gw_recv[mask - 1]
    bf_send[0] = mine
    row_copy(0).start()
    acc = backward(pairs // 3, 2 * pairs // 3, acc)
    row_copy(0).wait_recv()
    bf_send[1] = bf_send[0] + bf_recv[0]
    row_copy(1).start()
    acc = backward(2 * pairs // 3, pairs, acc)

    def section_sum(j, q):
        c = j * quart + q
        last = plan_ref[4 * pairs + c]
        some = plan_ref[4 * pairs + SECTIONS * quart + c]
        return jnp.where(some > 0, run[last], 0.0)

    def grad_copy(d):
        return remote(
            section(back_send, HALF + d), section(back_recv, HALF - d), d_send.at[HALF - d],
            d_recv.at[HALF - d], (row + d, rep),
        )

    for d in offsets:
        for q in range(quart):
            back_send[(HALF + d) * quart + q] = section_sum(HALF + d, q).astype(jnp.bfloat16)

        @pl.when(inside(d))
        def _():
            grad_copy(d).start()

    for k in range(1, len(bits)):
        row_copy(k).wait_recv()
        summed = bf_send[k] + bf_recv[k]
        if k + 1 < len(bits):
            bf_send[k + 1] = summed
            row_copy(k + 1).start()
    gw_all[pl.ds(rep * share, share)] = summed
    for mask in masks:
        gather_copy(mask, rep).start()

    for d in reversed(offsets):
        @pl.when(inside(d))
        def _():
            remote(
                section(back_send, HALF + d), section(back_recv, HALF + d), d_send.at[HALF + d],
                d_recv.at[HALF + d], (row + d, rep),
            ).wait_recv()
    for q in range(quart):
        result = section_sum(HALF, q)
        for d in offsets:
            result = result + back_recv[(HALF + d) * quart + q].astype(jnp.float32)
        grad_features_ref[q * blk:(q + 1) * blk] = result.T

    for mask in reversed(masks):
        gather_copy(mask, flip_all(rep, mask)).wait_recv()
    grad_weight_ref[...] = gw_all[...] * (rows * blocks * blk) ** (-0.5)

    for d in offsets:
        @pl.when(inside(d))
        def _():
            feature_copy(d).wait_send()
            grad_copy(d).wait_send()
    for mask in masks:
        part_copy(mask).wait_send()
        back_copy(mask, rep).wait_send()
        scatter_copy(mask).wait_send()
        gather_copy(mask, rep).wait_send()
    for k in range(len(bits)):
        row_copy(k).wait_send()


def make_plan(block_cols, quart):
    blocks, slots = block_cols.shape
    pairs = blocks * slots
    spots = SECTIONS * quart
    first = (lax.axis_index("row") - HALF) * blocks + lax.axis_index("rep") * quart
    moved = block_cols.reshape(pairs) - first
    slot = (moved // blocks) * quart + moved % blocks
    order = jnp.arange(pairs, dtype=jnp.int32)
    key = slot * pairs + order
    place = jnp.sum((key[None, :] < key[:, None]).astype(jnp.int32), axis=1)
    hot = (place[:, None] == order[None, :]).astype(jnp.int32)
    pair = jnp.sum(hot * order[:, None], axis=0)
    sorted_slot = jnp.sum(hot * slot[:, None], axis=0)
    same = (sorted_slot[1:] == sorted_slot[:-1]).astype(jnp.int32)
    keep = jnp.concatenate([jnp.zeros((1,), jnp.int32), same])
    spot = jnp.arange(spots, dtype=jnp.int32)
    ends = jnp.sum((slot[:, None] <= spot[None, :]).astype(jnp.int32), axis=0)
    some = jnp.sum((slot[:, None] == spot[None, :]).astype(jnp.int32), axis=0)
    last = jnp.maximum(ends - 1, 0)
    return jnp.concatenate([slot, pair, pair // slots, keep, last, some])


def on_device(rows, reps, features, block_cols, block_vals, weight, cotangent):
    group_rows, hidden = features.shape
    blocks, _, slots = block_cols.shape
    blk = block_vals.shape[-1]
    quart = blocks // reps
    pairs = blocks * slots
    own_rows = quart * blk
    steps = rows.bit_length() - 1
    share = hidden // reps
    plan = make_plan(block_cols[:, 0, :], quart)
    dma = pltpu.SemaphoreType.DMA
    bf16, f32 = jnp.bfloat16, jnp.float32
    vmem = pl.BlockSpec(memory_space=pltpu.VMEM)
    hbm = pl.BlockSpec(memory_space=pl.ANY)
    return pl.pallas_call(
        functools.partial(layer_kernel, (rows, reps, quart, slots, blk, blocks)),
        out_shape=(
            jax.ShapeDtypeStruct((own_rows, hidden), bf16),
            jax.ShapeDtypeStruct((hidden, hidden), f32),
            jax.ShapeDtypeStruct((own_rows, hidden), f32),
        ),
        in_specs=[pl.BlockSpec(memory_space=pltpu.SMEM), hbm, hbm, vmem, vmem],
        out_specs=(vmem, vmem, vmem),
        scratch_shapes=[
            pltpu.VMEM((pairs, blk, blk), bf16),
            pltpu.VMEM((SECTIONS * quart, blk, hidden), bf16),
            pltpu.VMEM((reps - 1, own_rows, hidden), bf16),
            pltpu.VMEM((reps - 1, own_rows, hidden), bf16),
            pltpu.VMEM((blocks, hidden, blk), bf16),
            pltpu.VMEM((pairs, hidden, blk), f32),
            pltpu.VMEM((SECTIONS * quart, hidden, blk), bf16),
            pltpu.VMEM((SECTIONS * quart, hidden, blk), bf16),
            pltpu.VMEM((hidden, hidden), f32),
            pltpu.VMEM((reps - 1, share, hidden), f32),
            pltpu.VMEM((steps, share, hidden), f32),
            pltpu.VMEM((steps, share, hidden), f32),
            pltpu.VMEM((hidden, hidden), f32),
            dma((2,)),
            dma((SECTIONS,)), dma((SECTIONS,)),
            dma((reps - 1,)), dma((reps - 1,)),
            dma((reps - 1,)), dma((reps - 1,)),
            dma((SECTIONS,)), dma((SECTIONS,)),
            dma((reps - 1,)), dma((reps - 1,)),
            dma((steps,)), dma((steps,)),
            dma((reps - 1,)), dma((reps - 1,)),
        ],
        compiler_params=pltpu.CompilerParams(
            collective_id=0, has_side_effects=True, vmem_limit_bytes=48 * 1024 * 1024
        ),
        cost_estimate=pl.CostEstimate(
            flops=4 * pairs * blk * blk * hidden, bytes_accessed=pairs * blk * blk * 2,
            transcendentals=own_rows * hidden,
        ),
    )(
        plan,
        features.reshape(blocks, blk, hidden),
        block_vals.reshape(pairs, blk, blk),
        weight,
        cotangent,
    )


def solution(mesh):
    return jax.shard_map(
        functools.partial(on_device, mesh.shape["row"], mesh.shape["rep"]),
        mesh=mesh,
        in_specs=(
            P("row", None),
            P("row", "rep", None),
            P("row", "rep", None, None, None),
            P(),
            P(("row", "rep"), None),
        ),
        out_specs=(P(("row", "rep"), None), P(), P(("row", "rep"), None)),
        check_vma=False,
    )
```

```python
import functools

import jax
import jax.numpy as jnp
from jax import lax
from jax.experimental import pallas as pl
from jax.experimental.pallas import tpu as pltpu
from jax.sharding import PartitionSpec as P

HALF = 3
SECTIONS = 2 * HALF + 1


def flip(index, bit):
    return index + bit * (1 - 2 * ((index // bit) % 2))


def flip_all(index, mask):
    bit = 1
    while bit <= mask:
        if mask & bit:
            index = flip(index, bit)
        bit *= 2
    return index


def remote(src, dst, send_sem, recv_sem, device):
    return pltpu.make_async_remote_copy(
        src_ref=src,
        dst_ref=dst,
        send_sem=send_sem,
        recv_sem=recv_sem,
        device_id=device,
        device_id_type=pl.DeviceIdType.MESH,
    )


def layer_kernel(
    sizes,
    plan_ref, features_ref, vals_ref, weight_ref, cotangent_ref,
    out_ref, grad_weight_ref, grad_features_ref,
    vals, turned, weight_own, cotangent, window, part_send, part_recv, back, run,
    back_send, back_recv, gw_send, gw_recv, bf_send, bf_recv, gw_all,
    local_sem, a_send, a_recv, b_send, b_recv, c_send, c_recv,
    d_send, d_recv, e_send, e_recv, f_send, f_recv, g_send, g_recv,
):
    rows, reps, quart, slots, blk, blocks = sizes
    pairs = blocks * slots
    spots = SECTIONS * quart
    padded = pairs + spots
    steps = padded // 2
    row = lax.axis_index("row")
    rep = lax.axis_index("rep")
    bits = [1 << k for k in range(rows.bit_length() - 1)]
    offsets = [d for d in (3, -3, 2, -2, 1, -1)]
    masks = sorted(range(1, reps), key=lambda m: -m)

    def inside(d):
        return jnp.logical_and(row + d >= 0, row + d < rows)

    vals_copy = pltpu.make_async_copy(vals_ref, vals, local_sem.at[0])
    vals_copy.start()
    weight_copy = pltpu.make_async_copy(weight_ref, weight_own, local_sem.at[2])
    weight_copy.start()
    cotangent_copy = pltpu.make_async_copy(cotangent_ref, cotangent, local_sem.at[3])
    cotangent_copy.start()
    own = features_ref.at[pl.ds(rep * quart, quart)]
    own_copy = pltpu.make_async_copy(own, window.at[pl.ds(HALF * quart, quart)], local_sem.at[1])
    own_copy.start()

    barrier = pltpu.get_barrier_semaphore()
    expected = reps - 1
    for d in offsets:
        @pl.when(inside(d))
        def _():
            pl.semaphore_signal(
                barrier, inc=1, device_id=(row + d, rep), device_id_type=pl.DeviceIdType.MESH
            )
        expected = expected + inside(d).astype(jnp.int32)
    for bit in bits:
        if bit > 2:
            pl.semaphore_signal(
                barrier, inc=1, device_id=(flip(row, bit), rep),
                device_id_type=pl.DeviceIdType.MESH,
            )
            expected = expected + 1
    for mask in masks:
        pl.semaphore_signal(
            barrier, inc=1, device_id=(row, flip_all(rep, mask)),
            device_id_type=pl.DeviceIdType.MESH,
        )
    pl.semaphore_wait(barrier, expected)

    def section(ref, j):
        return ref.at[pl.ds(j * quart, quart)]

    def feature_copy(d):
        return remote(
            own, section(window, HALF - d), a_send.at[HALF - d], a_recv.at[HALF - d],
            (row + d, rep),
        )

    for d in offsets:
        @pl.when(inside(d))
        def _():
            feature_copy(d).start()

        @pl.when(jnp.logical_not(inside(d)))
        def _():
            for q in range(quart):
                window[(HALF + d) * quart + q] = jnp.zeros(window.shape[1:], window.dtype)
                back_recv[(HALF + d) * quart + q] = jnp.zeros(
                    back_recv.shape[1:], back_recv.dtype
                )
    vals_copy.wait()

    turned[pairs] = jnp.zeros((blk, blk), turned.dtype)

    def turn(p, carry):
        turned[p] = vals[p].T
        return carry

    lax.fori_loop(0, pairs, turn, 0, unroll=8)
    own_copy.wait()
    weight_copy.wait()
    cotangent_copy.wait()
    for d in offsets:
        @pl.when(inside(d))
        def _():
            remote(
                own, section(window, HALF + d), a_send.at[HALF + d], a_recv.at[HALF + d],
                (row + d, rep),
            ).wait_recv()

    def partial(b):
        total = None
        for s in range(0, slots, 2):
            left = jnp.concatenate([vals[b * slots + s], vals[b * slots + s + 1]], axis=1)
            right = jnp.concatenate(
                [window[plan_ref[b * slots + s]], window[plan_ref[b * slots + s + 1]]], axis=0
            )
            term = jnp.dot(left, right, preferred_element_type=jnp.float32)
            total = term if total is None else total + term
        return total

    across, beside, opposite = flip(rep, 2), flip(rep, 1), flip_all(rep, 3)

    def partial_quarter(target):
        return jnp.concatenate([partial(target * quart + q) for q in range(quart)], axis=0)

    def part_copy(stage):
        return remote(
            part_send.at[stage], part_recv.at[stage], b_send.at[stage], b_recv.at[stage],
            (row, across if stage == 1 else beside),
        )

    part_send[0] = partial_quarter(opposite).astype(jnp.bfloat16)
    part_copy(0).start()
    total = partial_quarter(across)
    part_copy(0).wait_recv()
    part_send[1] = (total + part_recv[0].astype(jnp.float32)).astype(jnp.bfloat16)
    part_copy(1).start()
    part_send[2] = partial_quarter(beside).astype(jnp.bfloat16)
    part_copy(2).start()
    total = partial_quarter(rep)
    part_copy(2).wait_recv()
    total = total + part_recv[2].astype(jnp.float32)
    part_copy(1).wait_recv()
    total = total + part_recv[1].astype(jnp.float32)

    aggregate = total.astype(jnp.bfloat16)
    weight = weight_own[...]
    preact = jnp.dot(aggregate, weight, preferred_element_type=jnp.float32)
    sigmoid_pre = jax.nn.sigmoid(preact)
    grad_pre = (
        cotangent[...].astype(jnp.float32)
        * sigmoid_pre
        * (1.0 + preact * (1.0 - sigmoid_pre))
    ).astype(jnp.bfloat16)
    back_own = lax.dot_general(
        grad_pre, weight, (((1,), (1,)), ((), ())), preferred_element_type=jnp.float32
    ).astype(jnp.bfloat16)
    for q in range(quart):
        back[rep * quart + q] = back_own[q * blk:(q + 1) * blk]

    def back_copy(stage, owner):
        spot = section(back, owner)
        return remote(
            spot, spot, c_send.at[stage], c_recv.at[stage],
            (row, across if stage == 0 else beside),
        )

    back_copy(0, rep).start()
    back_copy(1, rep).start()
    out_ref[...] = (preact * sigmoid_pre).astype(jnp.bfloat16)

    gw_send[...] = lax.dot_general(
        aggregate, grad_pre, (((0,), (0,)), ((), ())), preferred_element_type=jnp.float32
    )
    share = gw_send.shape[0] // reps

    def share_of(ref, owner):
        return ref.at[pl.ds(owner * share, share)]

    def scatter_copy(mask):
        target = flip_all(rep, mask)
        return remote(
            share_of(gw_send, target), gw_recv.at[mask - 1], e_send.at[mask - 1],
            e_recv.at[mask - 1], (row, target),
        )

    def row_copy(k):
        return remote(
            bf_send.at[k], bf_recv.at[k], f_send.at[k], f_recv.at[k], (flip(row, bits[k]), rep)
        )

    def gather_copy(mask, owner):
        spot = share_of(gw_all, owner)
        return remote(
            spot, spot, g_send.at[mask - 1], g_recv.at[mask - 1], (row, flip_all(rep, mask))
        )

    for mask in masks:
        scatter_copy(mask).start()
    back_copy(0, across).wait_recv()
    back_copy(2, across).start()
    back_copy(1, beside).wait_recv()
    back_copy(2, opposite).wait_recv()

    def backward(start, stop, acc):
        def step(k, acc):
            left = jnp.concatenate(
                [turned[plan_ref[pairs + 2 * k]], turned[plan_ref[pairs + 2 * k + 1]]], axis=1
            )
            right = jnp.concatenate(
                [
                    back[plan_ref[pairs + padded + 2 * k]],
                    back[plan_ref[pairs + padded + 2 * k + 1]],
                ],
                axis=0,
            )
            keep = plan_ref[pairs + 2 * padded + k]
            term = jnp.dot(left, right, preferred_element_type=jnp.float32)
            acc = jnp.where(keep > 0, acc, 0.0) + term
            run[k] = acc
            return acc

        return lax.fori_loop(start, stop, step, acc, unroll=5)

    acc = jnp.zeros(run.shape[1:], jnp.float32)
    cuts = [0, steps // 15 * 5, steps // 15 * 10, steps]
    acc = backward(cuts[0], cuts[1], acc)
    mine = gw_send[pl.ds(rep * share, share)]
    for mask in reversed(masks):
        scatter_copy(mask).wait_recv()
        mine = mine + gw_recv[mask - 1]
    bf_send[0] = mine
    row_copy(0).start()
    acc = backward(cuts[1], cuts[2], acc)
    row_copy(0).wait_recv()
    bf_send[1] = bf_send[0] + bf_recv[0]
    row_copy(1).start()
    acc = backward(cuts[2], cuts[3], acc)

    def section_sum(j, q):
        c = j * quart + q
        last = plan_ref[pairs + 2 * padded + steps + c]
        some = plan_ref[pairs + 2 * padded + steps + spots + c]
        return jnp.where(some > 0, run[last], 0.0)

    def grad_copy(d):
        return remote(
            section(back_send, HALF + d), section(back_recv, HALF - d), d_send.at[HALF - d],
            d_recv.at[HALF - d], (row + d, rep),
        )

    for d in offsets:
        for q in range(quart):
            back_send[(HALF + d) * quart + q] = section_sum(HALF + d, q).astype(jnp.bfloat16)

        @pl.when(inside(d))
        def _():
            grad_copy(d).start()

    for k in range(1, len(bits)):
        row_copy(k).wait_recv()
        summed = bf_send[k] + bf_recv[k]
        if k + 1 < len(bits):
            bf_send[k + 1] = summed
            row_copy(k + 1).start()
    gw_all[pl.ds(rep * share, share)] = summed
    for mask in masks:
        gather_copy(mask, rep).start()

    for d in reversed(offsets):
        @pl.when(inside(d))
        def _():
            remote(
                section(back_send, HALF + d), section(back_recv, HALF + d), d_send.at[HALF + d],
                d_recv.at[HALF + d], (row + d, rep),
            ).wait_recv()
    for q in range(quart):
        result = section_sum(HALF, q)
        for d in offsets:
            result = result + back_recv[(HALF + d) * quart + q].astype(jnp.float32)
        grad_features_ref[q * blk:(q + 1) * blk] = result

    for mask in reversed(masks):
        gather_copy(mask, flip_all(rep, mask)).wait_recv()
    grad_weight_ref[...] = gw_all[...] * (rows * blocks * blk) ** (-0.5)

    for d in offsets:
        @pl.when(inside(d))
        def _():
            feature_copy(d).wait_send()
            grad_copy(d).wait_send()
    for mask in masks:
        part_copy(mask - 1).wait_send()
        back_copy(mask - 1, rep).wait_send()
        scatter_copy(mask).wait_send()
        gather_copy(mask, rep).wait_send()
    for k in range(len(bits)):
        row_copy(k).wait_send()


def make_plan(block_cols, quart):
    blocks, slots = block_cols.shape
    pairs = blocks * slots
    spots = SECTIONS * quart
    first = (lax.axis_index("row") - HALF) * blocks + lax.axis_index("rep") * quart
    moved = block_cols.reshape(pairs) - first
    slot = (moved // blocks) * quart + moved % blocks
    order = jnp.arange(pairs, dtype=jnp.int32)
    spot = jnp.arange(spots, dtype=jnp.int32)
    count = jnp.sum((slot[:, None] == spot[None, :]).astype(jnp.int32), axis=0)
    width = (count + 1) // 2
    start = jnp.sum(jnp.where(spot[:, None] < spot[None, :], width[:, None], 0), axis=0)
    rank = jnp.sum(
        ((slot[:, None] == slot[None, :]) & (order[:, None] < order[None, :])).astype(jnp.int32),
        axis=0,
    )
    base = jnp.sum(jnp.where(spot[None, :] == slot[:, None], start[None, :], 0), axis=1)
    place = 2 * base + rank
    hot = place[:, None] == jnp.arange(pairs + spots, dtype=jnp.int32)[None, :]
    pair = pairs + jnp.sum(jnp.where(hot, order[:, None] - pairs, 0), axis=0)
    block = jnp.sum(jnp.where(hot, order[:, None] // slots, 0), axis=0)
    step = jnp.arange((pairs + spots) // 2, dtype=jnp.int32)
    first_of = (start[:, None] == step[None, :]) & (count[:, None] > 0)
    keep = 1 - jnp.sum(first_of.astype(jnp.int32), axis=0)
    last = jnp.maximum(start + width - 1, 0)
    return jnp.concatenate([slot, pair, block, keep, last, count])


def on_device(rows, reps, features, block_cols, block_vals, weight, cotangent):
    group_rows, hidden = features.shape
    blocks, _, slots = block_cols.shape
    blk = block_vals.shape[-1]
    quart = blocks // reps
    pairs = blocks * slots
    own_rows = quart * blk
    levels = rows.bit_length() - 1
    share = hidden // reps
    plan = make_plan(block_cols[:, 0, :], quart)
    dma = pltpu.SemaphoreType.DMA
    bf16, f32 = jnp.bfloat16, jnp.float32
    vmem = pl.BlockSpec(memory_space=pltpu.VMEM)
    hbm = pl.BlockSpec(memory_space=pl.ANY)
    return pl.pallas_call(
        functools.partial(layer_kernel, (rows, reps, quart, slots, blk, blocks)),
        out_shape=(
            jax.ShapeDtypeStruct((own_rows, hidden), bf16),
            jax.ShapeDtypeStruct((hidden, hidden), f32),
            jax.ShapeDtypeStruct((own_rows, hidden), f32),
        ),
        in_specs=[pl.BlockSpec(memory_space=pltpu.SMEM), hbm, hbm, hbm, hbm],
        out_specs=(vmem, vmem, vmem),
        scratch_shapes=[
            pltpu.VMEM((pairs, blk, blk), bf16),
            pltpu.VMEM((pairs + 1, blk, blk), bf16),
            pltpu.VMEM((hidden, hidden), bf16),
            pltpu.VMEM((own_rows, hidden), bf16),
            pltpu.VMEM((SECTIONS * quart, blk, hidden), bf16),
            pltpu.VMEM((reps - 1, own_rows, hidden), bf16),
            pltpu.VMEM((reps - 1, own_rows, hidden), bf16),
            pltpu.VMEM((blocks, blk, hidden), bf16),
            pltpu.VMEM(((pairs + SECTIONS * quart) // 2, blk, hidden), f32),
            pltpu.VMEM((SECTIONS * quart, blk, hidden), bf16),
            pltpu.VMEM((SECTIONS * quart, blk, hidden), bf16),
            pltpu.VMEM((hidden, hidden), f32),
            pltpu.VMEM((reps - 1, share, hidden), f32),
            pltpu.VMEM((levels, share, hidden), f32),
            pltpu.VMEM((levels, share, hidden), f32),
            pltpu.VMEM((hidden, hidden), f32),
            dma((4,)),
            dma((SECTIONS,)), dma((SECTIONS,)),
            dma((reps - 1,)), dma((reps - 1,)),
            dma((reps - 1,)), dma((reps - 1,)),
            dma((SECTIONS,)), dma((SECTIONS,)),
            dma((reps - 1,)), dma((reps - 1,)),
            dma((levels,)), dma((levels,)),
            dma((reps - 1,)), dma((reps - 1,)),
        ],
        compiler_params=pltpu.CompilerParams(
            collective_id=0, has_side_effects=True, vmem_limit_bytes=60 * 1024 * 1024
        ),
        cost_estimate=pl.CostEstimate(
            flops=4 * pairs * blk * blk * hidden, bytes_accessed=pairs * blk * blk * 2,
            transcendentals=own_rows * hidden,
        ),
    )(
        plan,
        features.reshape(blocks, blk, hidden),
        block_vals.reshape(pairs, blk, blk),
        weight,
        cotangent,
    )


def solution(mesh):
    return jax.shard_map(
        functools.partial(on_device, mesh.shape["row"], mesh.shape["rep"]),
        mesh=mesh,
        in_specs=(
            P("row", None),
            P("row", "rep", None),
            P("row", "rep", None, None, None),
            P(),
            P(("row", "rep"), None),
        ),
        out_specs=(P(("row", "rep"), None), P(), P(("row", "rep"), None)),
        check_vma=False,
    )
```

```python
import functools

import jax
import jax.numpy as jnp
from jax import lax
from jax.experimental import pallas as pl
from jax.experimental.pallas import tpu as pltpu
from jax.sharding import PartitionSpec as P

HALF = 3
SECTIONS = 2 * HALF + 1


def flip(index, bit):
    return index + bit * (1 - 2 * ((index // bit) % 2))


def flip_all(index, mask):
    bit = 1
    while bit <= mask:
        if mask & bit:
            index = flip(index, bit)
        bit *= 2
    return index


def remote(src, dst, send_sem, recv_sem, device):
    return pltpu.make_async_remote_copy(
        src_ref=src,
        dst_ref=dst,
        send_sem=send_sem,
        recv_sem=recv_sem,
        device_id=device,
        device_id_type=pl.DeviceIdType.MESH,
    )


def layer_kernel(
    sizes,
    plan_ref, features_ref, vals_ref, weight_ref, cotangent_ref,
    out_ref, grad_weight_ref, grad_features_ref,
    vals, turned, weight_own, cotangent, window, part_send, part_recv, near, far, run,
    back_send, back_recv, gw_send, gw_recv, gw_half, gw_across, bf_send, bf_recv, gw_all,
    local_sem, a_send, a_recv, b_send, b_recv, c_send, c_recv,
    d_send, d_recv, e_send, e_recv, f_send, f_recv, g_send, g_recv,
):
    rows, reps, quart, slots, blk, blocks = sizes
    pairs = blocks * slots
    spots = SECTIONS * quart
    padded = pairs + 2 * spots
    steps = padded // 2
    row = lax.axis_index("row")
    rep = lax.axis_index("rep")
    bits = [1 << k for k in range(rows.bit_length() - 1)]
    offsets = [d for d in (3, -3, 2, -2, 1, -1)]
    masks = sorted(range(1, reps), key=lambda m: -m)

    def inside(d):
        return jnp.logical_and(row + d >= 0, row + d < rows)

    vals_copy = pltpu.make_async_copy(vals_ref, vals, local_sem.at[0])
    vals_copy.start()
    weight_copy = pltpu.make_async_copy(weight_ref, weight_own, local_sem.at[2])
    weight_copy.start()
    cotangent_copy = pltpu.make_async_copy(cotangent_ref, cotangent, local_sem.at[3])
    cotangent_copy.start()
    own = features_ref.at[pl.ds(rep * quart, quart)]
    own_copy = pltpu.make_async_copy(own, window.at[pl.ds(HALF * quart, quart)], local_sem.at[1])
    own_copy.start()

    barrier = pltpu.get_barrier_semaphore()
    expected = reps - 1
    for d in offsets:
        @pl.when(inside(d))
        def _():
            pl.semaphore_signal(
                barrier, inc=1, device_id=(row + d, rep), device_id_type=pl.DeviceIdType.MESH
            )
        expected = expected + inside(d).astype(jnp.int32)
    for bit in bits:
        if bit > 2:
            pl.semaphore_signal(
                barrier, inc=1, device_id=(flip(row, bit), rep),
                device_id_type=pl.DeviceIdType.MESH,
            )
            expected = expected + 1
    for mask in masks:
        pl.semaphore_signal(
            barrier, inc=1, device_id=(row, flip_all(rep, mask)),
            device_id_type=pl.DeviceIdType.MESH,
        )
    pl.semaphore_wait(barrier, expected)

    def section(ref, j):
        return ref.at[pl.ds(j * quart, quart)]

    def feature_copy(d):
        return remote(
            own, section(window, HALF - d), a_send.at[HALF - d], a_recv.at[HALF - d],
            (row + d, rep),
        )

    for d in offsets:
        @pl.when(inside(d))
        def _():
            feature_copy(d).start()

        @pl.when(jnp.logical_not(inside(d)))
        def _():
            for q in range(quart):
                window[(HALF + d) * quart + q] = jnp.zeros(window.shape[1:], window.dtype)
                back_recv[(HALF + d) * quart + q] = jnp.zeros(
                    back_recv.shape[1:], back_recv.dtype
                )
    vals_copy.wait()

    turned[pairs] = jnp.zeros((blk, blk), turned.dtype)

    def turn(p, carry):
        turned[p] = vals[p].T
        return carry

    lax.fori_loop(0, pairs, turn, 0, unroll=8)
    own_copy.wait()
    weight_copy.wait()
    cotangent_copy.wait()
    for d in offsets:
        @pl.when(inside(d))
        def _():
            remote(
                own, section(window, HALF + d), a_send.at[HALF + d], a_recv.at[HALF + d],
                (row + d, rep),
            ).wait_recv()

    def partial(b):
        total = None
        for s in range(0, slots, 2):
            left = jnp.concatenate([vals[b * slots + s], vals[b * slots + s + 1]], axis=1)
            right = jnp.concatenate(
                [window[plan_ref[b * slots + s]], window[plan_ref[b * slots + s + 1]]], axis=0
            )
            term = jnp.dot(left, right, preferred_element_type=jnp.float32)
            total = term if total is None else total + term
        return total

    across, beside, opposite = flip(rep, 2), flip(rep, 1), flip_all(rep, 3)

    def partial_quarter(target):
        return jnp.concatenate([partial(target * quart + q) for q in range(quart)], axis=0)

    def part_copy(stage):
        return remote(
            part_send.at[stage], part_recv.at[stage], b_send.at[stage], b_recv.at[stage],
            (row, across if stage == 1 else beside),
        )

    part_send[0] = partial_quarter(opposite).astype(jnp.bfloat16)
    part_copy(0).start()
    total = partial_quarter(across)
    part_copy(0).wait_recv()
    part_send[1] = (total + part_recv[0].astype(jnp.float32)).astype(jnp.bfloat16)
    part_copy(1).start()
    part_send[2] = partial_quarter(beside).astype(jnp.bfloat16)
    part_copy(2).start()
    total = partial_quarter(rep)
    part_copy(2).wait_recv()
    total = total + part_recv[2].astype(jnp.float32)
    part_copy(1).wait_recv()
    total = total + part_recv[1].astype(jnp.float32)

    aggregate = total.astype(jnp.bfloat16)
    weight = weight_own[...]
    preact = jnp.dot(aggregate, weight, preferred_element_type=jnp.float32)
    sigmoid_pre = jax.nn.sigmoid(preact)
    grad_pre = (
        cotangent[...].astype(jnp.float32)
        * sigmoid_pre
        * (1.0 + preact * (1.0 - sigmoid_pre))
    ).astype(jnp.bfloat16)
    back_own = lax.dot_general(
        grad_pre, weight, (((1,), (1,)), ((), ())), preferred_element_type=jnp.float32
    ).astype(jnp.bfloat16)
    core, chip = rep % 2, rep // 2
    for q in range(quart):
        near[core * quart + q] = back_own[q * blk:(q + 1) * blk]

    def back_copy(stage):
        src, dst, target = ((near, far, across), (near, near, beside), (far, far, beside))[stage]
        return remote(
            section(src, core), section(dst, core), c_send.at[stage], c_recv.at[stage],
            (row, target),
        )

    back_copy(0).start()
    back_copy(1).start()
    out_ref[...] = (preact * sigmoid_pre).astype(jnp.bfloat16)

    gw_send[...] = lax.dot_general(
        aggregate, grad_pre, (((0,), (0,)), ((), ())), preferred_element_type=jnp.float32
    )
    half_rows = gw_send.shape[0] // 2
    share = half_rows // 2

    def share_of(ref, owner):
        return ref.at[pl.ds(((owner % 2) * 2 + owner // 2) * share, share)]

    def beside_copy():
        return remote(
            gw_send.at[pl.ds((1 - core) * half_rows, half_rows)], gw_recv,
            e_send.at[0], e_recv.at[0], (row, beside),
        )

    def across_copy():
        return remote(
            gw_half.at[pl.ds((1 - chip) * share, share)], gw_across,
            e_send.at[1], e_recv.at[1], (row, across),
        )

    def row_copy(k):
        return remote(
            bf_send.at[k], bf_recv.at[k], f_send.at[k], f_recv.at[k], (flip(row, bits[k]), rep)
        )

    def gather_copy(mask, owner):
        spot = share_of(gw_all, owner)
        return remote(
            spot, spot, g_send.at[mask - 1], g_recv.at[mask - 1], (row, flip_all(rep, mask))
        )

    beside_copy().start()
    beside_copy().wait_recv()
    gw_half[...] = gw_send[pl.ds(core * half_rows, half_rows)] + gw_recv[...]
    across_copy().start()
    back_copy(1).wait_recv()

    def backward(source, start, stop, acc):
        def step(k, acc):
            left = jnp.concatenate(
                [turned[plan_ref[pairs + 2 * k]], turned[plan_ref[pairs + 2 * k + 1]]], axis=1
            )
            right = jnp.concatenate(
                [
                    source[plan_ref[pairs + padded + 2 * k]],
                    source[plan_ref[pairs + padded + 2 * k + 1]],
                ],
                axis=0,
            )
            keep = plan_ref[pairs + 2 * padded + k]
            term = jnp.dot(left, right, preferred_element_type=jnp.float32)
            acc = jnp.where(keep > 0, acc, 0.0) + term
            run[k] = acc
            return acc

        return lax.fori_loop(start, stop, step, acc, unroll=5)

    zeros = jnp.zeros(run.shape[1:], jnp.float32)
    half = steps // 2
    fifth = half // 10 * 5
    acc = backward(near, 0, fifth, zeros)
    back_copy(0).wait_recv()
    back_copy(2).start()
    across_copy().wait_recv()
    bf_send[0] = gw_half[pl.ds(chip * share, share)] + gw_across[...]
    row_copy(0).start()
    backward(near, fifth, half, acc)
    back_copy(2).wait_recv()
    row_copy(0).wait_recv()
    bf_send[1] = bf_send[0] + bf_recv[0]
    row_copy(1).start()
    acc = backward(far, half, half + fifth, zeros)
    row_copy(1).wait_recv()
    bf_send[2] = bf_send[1] + bf_recv[1]
    row_copy(2).start()
    backward(far, half + fifth, steps, acc)

    def section_sum(j, q):
        found = []
        for c in (j * quart + q, spots + j * quart + q):
            last = plan_ref[pairs + 2 * padded + steps + c]
            some = plan_ref[pairs + 2 * padded + steps + 2 * spots + c]
            found.append(jnp.where(some > 0, run[last], 0.0))
        return found[0] + found[1]

    def grad_copy(d):
        return remote(
            section(back_send, HALF + d), section(back_recv, HALF - d), d_send.at[HALF - d],
            d_recv.at[HALF - d], (row + d, rep),
        )

    for d in offsets:
        for q in range(quart):
            back_send[(HALF + d) * quart + q] = section_sum(HALF + d, q).astype(jnp.bfloat16)

        @pl.when(inside(d))
        def _():
            grad_copy(d).start()

    for k in range(2, len(bits)):
        row_copy(k).wait_recv()
        summed = bf_send[k] + bf_recv[k]
        if k + 1 < len(bits):
            bf_send[k + 1] = summed
            row_copy(k + 1).start()
    gw_all[pl.ds((core * 2 + chip) * share, share)] = summed
    for mask in masks:
        gather_copy(mask, rep).start()

    for d in reversed(offsets):
        @pl.when(inside(d))
        def _():
            remote(
                section(back_send, HALF + d), section(back_recv, HALF + d), d_send.at[HALF + d],
                d_recv.at[HALF + d], (row + d, rep),
            ).wait_recv()
    for q in range(quart):
        result = section_sum(HALF, q)
        for d in offsets:
            result = result + back_recv[(HALF + d) * quart + q].astype(jnp.float32)
        grad_features_ref[q * blk:(q + 1) * blk] = result

    for mask in reversed(masks):
        gather_copy(mask, flip_all(rep, mask)).wait_recv()
    grad_weight_ref[...] = gw_all[...] * (rows * blocks * blk) ** (-0.5)

    for d in offsets:
        @pl.when(inside(d))
        def _():
            feature_copy(d).wait_send()
            grad_copy(d).wait_send()
    for mask in masks:
        part_copy(mask - 1).wait_send()
        back_copy(mask - 1).wait_send()
        gather_copy(mask, rep).wait_send()
    beside_copy().wait_send()
    across_copy().wait_send()
    for k in range(len(bits)):
        row_copy(k).wait_send()


def store_kernel(a_ref, b_ref, c_ref, a_out, b_out, c_out, sems):
    copies = [
        pltpu.make_async_copy(src, dst, sems.at[k])
        for k, (src, dst) in enumerate(((a_ref, a_out), (b_ref, b_out), (c_ref, c_out)))
    ]
    for copy in copies:
        copy.start()
    for copy in copies:
        copy.wait()


def make_plan(block_cols, quart):
    blocks, slots = block_cols.shape
    pairs = blocks * slots
    spots = SECTIONS * quart
    first = (lax.axis_index("row") - HALF) * blocks + lax.axis_index("rep") * quart
    moved = block_cols.reshape(pairs) - first
    slot = (moved // blocks) * quart + moved % blocks
    order = jnp.arange(pairs, dtype=jnp.int32)
    far = (order // slots // quart) // 2 != lax.axis_index("rep") // 2
    bin_of = slot + jnp.where(far, spots, 0)
    spot = jnp.arange(2 * spots, dtype=jnp.int32)
    half = (pairs // 2 + spots) // 2
    count = jnp.sum((bin_of[:, None] == spot[None, :]).astype(jnp.int32), axis=0)
    width = (count + 1) // 2
    same_half = (spot[:, None] // spots) == (spot[None, :] // spots)
    before = same_half & (spot[:, None] < spot[None, :])
    start = jnp.sum(jnp.where(before, width[:, None], 0), axis=0) + half * (spot // spots)
    rank = jnp.sum(
        ((bin_of[:, None] == bin_of[None, :]) & (order[:, None] < order[None, :])).astype(
            jnp.int32
        ),
        axis=0,
    )
    base = jnp.sum(jnp.where(spot[None, :] == bin_of[:, None], start[None, :], 0), axis=1)
    place = 2 * base + rank
    hot = place[:, None] == jnp.arange(4 * half, dtype=jnp.int32)[None, :]
    pair = pairs + jnp.sum(jnp.where(hot, order[:, None] - pairs, 0), axis=0)
    block = jnp.sum(jnp.where(hot, order[:, None] // slots % (2 * quart), 0), axis=0)
    step = jnp.arange(2 * half, dtype=jnp.int32)
    first_of = (start[:, None] == step[None, :]) & (count[:, None] > 0)
    keep = 1 - jnp.sum(first_of.astype(jnp.int32), axis=0)
    last = jnp.maximum(start + width - 1, 0)
    return jnp.concatenate([slot, pair, block, keep, last, count])


def on_device(rows, reps, features, block_cols, block_vals, weight, cotangent):
    group_rows, hidden = features.shape
    blocks, _, slots = block_cols.shape
    blk = block_vals.shape[-1]
    quart = blocks // reps
    pairs = blocks * slots
    own_rows = quart * blk
    levels = rows.bit_length() - 1
    share = hidden // reps
    plan = make_plan(block_cols[:, 0, :], quart)
    dma = pltpu.SemaphoreType.DMA
    bf16, f32 = jnp.bfloat16, jnp.float32
    vmem = pl.BlockSpec(memory_space=pltpu.VMEM)
    hbm = pl.BlockSpec(memory_space=pl.ANY)
    results = pl.pallas_call(
        functools.partial(layer_kernel, (rows, reps, quart, slots, blk, blocks)),
        out_shape=(
            jax.ShapeDtypeStruct((own_rows, hidden), bf16),
            jax.ShapeDtypeStruct((hidden, hidden), f32),
            jax.ShapeDtypeStruct((own_rows, hidden), f32),
        ),
        in_specs=[pl.BlockSpec(memory_space=pltpu.SMEM), hbm, hbm, hbm, hbm],
        out_specs=(vmem, vmem, vmem),
        scratch_shapes=[
            pltpu.VMEM((pairs, blk, blk), bf16),
            pltpu.VMEM((pairs + 1, blk, blk), bf16),
            pltpu.VMEM((hidden, hidden), bf16),
            pltpu.VMEM((own_rows, hidden), bf16),
            pltpu.VMEM((SECTIONS * quart, blk, hidden), bf16),
            pltpu.VMEM((reps - 1, own_rows, hidden), bf16),
            pltpu.VMEM((reps - 1, own_rows, hidden), bf16),
            pltpu.VMEM((blocks // 2, blk, hidden), bf16),
            pltpu.VMEM((blocks // 2, blk, hidden), bf16),
            pltpu.VMEM((pairs // 2 + SECTIONS * quart, blk, hidden), f32),
            pltpu.VMEM((SECTIONS * quart, blk, hidden), bf16),
            pltpu.VMEM((SECTIONS * quart, blk, hidden), bf16),
            pltpu.VMEM((hidden, hidden), f32),
            pltpu.VMEM((2 * share, hidden), f32),
            pltpu.VMEM((2 * share, hidden), f32),
            pltpu.VMEM((share, hidden), f32),
            pltpu.VMEM((levels, share, hidden), f32),
            pltpu.VMEM((levels, share, hidden), f32),
            pltpu.VMEM((hidden, hidden), f32),
            dma((4,)),
            dma((SECTIONS,)), dma((SECTIONS,)),
            dma((reps - 1,)), dma((reps - 1,)),
            dma((reps - 1,)), dma((reps - 1,)),
            dma((SECTIONS,)), dma((SECTIONS,)),
            dma((reps - 1,)), dma((reps - 1,)),
            dma((levels,)), dma((levels,)),
            dma((reps - 1,)), dma((reps - 1,)),
        ],
        compiler_params=pltpu.CompilerParams(
            collective_id=0, has_side_effects=True, vmem_limit_bytes=60 * 1024 * 1024
        ),
        cost_estimate=pl.CostEstimate(
            flops=4 * pairs * blk * blk * hidden, bytes_accessed=pairs * blk * blk * 2,
            transcendentals=own_rows * hidden,
        ),
    )(
        plan,
        features.reshape(blocks, blk, hidden),
        block_vals.reshape(pairs, blk, blk),
        weight,
        cotangent,
    )
    return pl.pallas_call(
        store_kernel,
        out_shape=tuple(jax.ShapeDtypeStruct(r.shape, r.dtype) for r in results),
        in_specs=[hbm, hbm, hbm],
        out_specs=(hbm, hbm, hbm),
        scratch_shapes=[dma((3,))],
        compiler_params=pltpu.CompilerParams(vmem_limit_bytes=60 * 1024 * 1024),
        cost_estimate=pl.CostEstimate(
            flops=0, bytes_accessed=20 * own_rows * hidden, transcendentals=0
        ),
    )(*results)


def solution(mesh):
    return jax.shard_map(
        functools.partial(on_device, mesh.shape["row"], mesh.shape["rep"]),
        mesh=mesh,
        in_specs=(
            P("row", None),
            P("row", "rep", None),
            P("row", "rep", None, None, None),
            P(),
            P(("row", "rep"), None),
        ),
        out_specs=(P(("row", "rep"), None), P(), P(("row", "rep"), None)),
        check_vma=False,
    )
```

```python
import functools

import jax
import jax.numpy as jnp
from jax import lax
from jax.experimental import pallas as pl
from jax.experimental.pallas import tpu as pltpu
from jax.sharding import PartitionSpec as P

HALF = 3
SECTIONS = 2 * HALF + 1


def flip(index, bit):
    return index + bit * (1 - 2 * ((index // bit) % 2))


def flip_all(index, mask):
    bit = 1
    while bit <= mask:
        if mask & bit:
            index = flip(index, bit)
        bit *= 2
    return index


def remote(src, dst, send_sem, recv_sem, device):
    return pltpu.make_async_remote_copy(
        src_ref=src,
        dst_ref=dst,
        send_sem=send_sem,
        recv_sem=recv_sem,
        device_id=device,
        device_id_type=pl.DeviceIdType.MESH,
    )


def layer_kernel(
    sizes,
    plan_ref, features_ref, vals_ref, weight_ref, cotangent_ref,
    out_ref, grad_weight_ref, grad_features_ref,
    vals, turned, weight_own, cotangent, window, part_send, part_recv, near, far, run,
    back_send, back_recv, gw_send, gw_recv, gw_half, gw_across, bf_send, bf_recv, gw_all,
    local_sem, a_send, a_recv, b_send, b_recv, c_send, c_recv,
    d_send, d_recv, e_send, e_recv, f_send, f_recv, g_send, g_recv,
):
    rows, reps, quart, slots, blk, blocks = sizes
    pairs = blocks * slots
    spots = SECTIONS * quart
    padded = pairs + 2 * spots
    steps = padded // 2
    row = lax.axis_index("row")
    rep = lax.axis_index("rep")
    bits = [1 << k for k in range(rows.bit_length() - 1)]
    offsets = [d for d in (3, -3, 2, -2, 1, -1)]
    masks = sorted(range(1, reps), key=lambda m: -m)

    def inside(d):
        return jnp.logical_and(row + d >= 0, row + d < rows)

    vals_copy = pltpu.make_async_copy(vals_ref, vals, local_sem.at[0])
    vals_copy.start()
    weight_copy = pltpu.make_async_copy(weight_ref, weight_own, local_sem.at[2])
    weight_copy.start()
    cotangent_copy = pltpu.make_async_copy(cotangent_ref, cotangent, local_sem.at[3])
    cotangent_copy.start()
    own = features_ref.at[pl.ds(rep * quart, quart)]
    own_copy = pltpu.make_async_copy(own, window.at[pl.ds(HALF * quart, quart)], local_sem.at[1])
    own_copy.start()

    barrier = pltpu.get_barrier_semaphore()
    expected = reps - 1
    for d in offsets:
        @pl.when(inside(d))
        def _():
            pl.semaphore_signal(
                barrier, inc=1, device_id=(row + d, rep), device_id_type=pl.DeviceIdType.MESH
            )
        expected = expected + inside(d).astype(jnp.int32)
    for bit in bits:
        if bit > 2:
            pl.semaphore_signal(
                barrier, inc=1, device_id=(flip(row, bit), rep),
                device_id_type=pl.DeviceIdType.MESH,
            )
            expected = expected + 1
    for mask in masks:
        pl.semaphore_signal(
            barrier, inc=1, device_id=(row, flip_all(rep, mask)),
            device_id_type=pl.DeviceIdType.MESH,
        )
    pl.semaphore_wait(barrier, expected)

    def section(ref, j):
        return ref.at[pl.ds(j * quart, quart)]

    side = 1 - 2 * (row % 2)
    odd = row % 2
    peer = row + side
    first = quart // 2

    def piece(off, part):
        start, size = ((0, quart), (0, first), (first, quart - first))[part]
        return window.at[pl.ds((HALF + off) * quart + start, size)]

    def feature_copy(k):
        src, dst, target = (
            (own, piece(-side, 0), peer),
            (own, piece(-2, 0), row + 2),
            (own, piece(2, 0), row - 2),
            (piece(side, 1), piece(side - 2, 1), row + 2),
            (piece(side, 1), piece(side + 2, 1), row - 2),
            (piece(2, 2), piece(2 - side, 2), peer),
            (piece(-2, 2), piece(-2 - side, 2), peer),
            (piece(-side, 0), piece(-3 * side, 0), row + 2 * side),
        )[k]
        return remote(src, dst, a_send.at[k], a_recv.at[k], (target, rep))

    def feature_wait(sem, part):
        spot = piece(0, part)
        remote(spot, spot, a_send.at[0], a_recv.at[sem], (peer, rep)).wait_recv()

    above, below = inside(2), inside(-2)
    sends = (
        None, above, below, above, below, above, below,
        jnp.logical_and(inside(-side), inside(2 * side)),
    )

    def start_feature(k):
        if sends[k] is None:
            feature_copy(k).start()
        else:
            @pl.when(sends[k])
            def _():
                feature_copy(k).start()

    for k in (0, 1, 2):
        start_feature(k)
    vals_copy.wait()

    turned[pairs] = jnp.zeros((blk, blk), turned.dtype)

    def turn(p, carry):
        turned[p] = vals[p].T
        return carry

    lax.fori_loop(0, pairs // 2, turn, 0, unroll=8)
    feature_wait(0, 0)
    start_feature(3)
    start_feature(4)

    @pl.when(above)
    def _():
        feature_wait(2, 0)

    start_feature(5)

    @pl.when(below)
    def _():
        feature_wait(1, 0)

    start_feature(6)
    lax.fori_loop(pairs // 2, pairs, turn, 0, unroll=8)

    @pl.when(inside(-side))
    def _():
        feature_wait(3 + odd, 1)
        feature_wait(6 - odd, 2)

    start_feature(7)
    for d in offsets:
        @pl.when(jnp.logical_not(inside(d)))
        def _():
            for q in range(quart):
                window[(HALF + d) * quart + q] = jnp.zeros(window.shape[1:], window.dtype)
                back_recv[(HALF + d) * quart + q] = jnp.zeros(
                    back_recv.shape[1:], back_recv.dtype
                )
    own_copy.wait()
    weight_copy.wait()
    cotangent_copy.wait()

    @pl.when(inside(3 * side))
    def _():
        feature_wait(4 - odd, 1)
        feature_wait(5 + odd, 2)

    @pl.when(inside(-3 * side))
    def _():
        feature_wait(7, 0)

    def partial(b):
        total = None
        for s in range(0, slots, 2):
            left = jnp.concatenate([vals[b * slots + s], vals[b * slots + s + 1]], axis=1)
            right = jnp.concatenate(
                [window[plan_ref[b * slots + s]], window[plan_ref[b * slots + s + 1]]], axis=0
            )
            term = jnp.dot(left, right, preferred_element_type=jnp.float32)
            total = term if total is None else total + term
        return total

    across, beside, opposite = flip(rep, 2), flip(rep, 1), flip_all(rep, 3)

    def partial_quarter(target):
        return jnp.concatenate([partial(target * quart + q) for q in range(quart)], axis=0)

    def part_copy(stage):
        return remote(
            part_send.at[stage], part_recv.at[stage], b_send.at[stage], b_recv.at[stage],
            (row, across if stage == 1 else beside),
        )

    part_send[0] = partial_quarter(opposite).astype(jnp.bfloat16)
    part_copy(0).start()
    total = partial_quarter(across)
    part_copy(0).wait_recv()
    part_send[1] = (total + part_recv[0].astype(jnp.float32)).astype(jnp.bfloat16)
    part_copy(1).start()
    part_send[2] = partial_quarter(beside).astype(jnp.bfloat16)
    part_copy(2).start()
    total = partial_quarter(rep)
    part_copy(2).wait_recv()
    total = total + part_recv[2].astype(jnp.float32)
    part_copy(1).wait_recv()
    total = total + part_recv[1].astype(jnp.float32)

    aggregate = total.astype(jnp.bfloat16)
    weight = weight_own[...]
    preact = jnp.dot(aggregate, weight, preferred_element_type=jnp.float32)
    sigmoid_pre = jax.nn.sigmoid(preact)
    grad_pre = (
        cotangent[...].astype(jnp.float32)
        * sigmoid_pre
        * (1.0 + preact * (1.0 - sigmoid_pre))
    ).astype(jnp.bfloat16)
    back_own = lax.dot_general(
        grad_pre, weight, (((1,), (1,)), ((), ())), preferred_element_type=jnp.float32
    ).astype(jnp.bfloat16)
    core, chip = rep % 2, rep // 2
    for q in range(quart):
        near[core * quart + q] = back_own[q * blk:(q + 1) * blk]

    def back_copy(stage):
        src, dst, target = ((near, far, across), (near, near, beside), (far, far, beside))[stage]
        return remote(
            section(src, core), section(dst, core), c_send.at[stage], c_recv.at[stage],
            (row, target),
        )

    back_copy(0).start()
    back_copy(1).start()
    out_ref[...] = (preact * sigmoid_pre).astype(jnp.bfloat16)

    gw_send[...] = lax.dot_general(
        aggregate, grad_pre, (((0,), (0,)), ((), ())), preferred_element_type=jnp.float32
    )
    half_rows = gw_send.shape[0] // 2
    share = half_rows // 2

    def share_of(ref, owner):
        return ref.at[pl.ds(((owner % 2) * 2 + owner // 2) * share, share)]

    def beside_copy():
        return remote(
            gw_send.at[pl.ds((1 - core) * half_rows, half_rows)], gw_recv,
            e_send.at[0], e_recv.at[0], (row, beside),
        )

    def across_copy():
        return remote(
            gw_half.at[pl.ds((1 - chip) * share, share)], gw_across,
            e_send.at[1], e_recv.at[1], (row, across),
        )

    def row_copy(k):
        return remote(
            bf_send.at[k], bf_recv.at[k], f_send.at[k], f_recv.at[k], (flip(row, bits[k]), rep)
        )

    def gather_copy(mask, owner):
        spot = share_of(gw_all, owner)
        return remote(
            spot, spot, g_send.at[mask - 1], g_recv.at[mask - 1], (row, flip_all(rep, mask))
        )

    beside_copy().start()
    beside_copy().wait_recv()
    gw_half[...] = gw_send[pl.ds(core * half_rows, half_rows)] + gw_recv[...]
    across_copy().start()
    back_copy(1).wait_recv()

    def backward(source, start, stop, acc):
        def step(k, acc):
            left = jnp.concatenate(
                [turned[plan_ref[pairs + 2 * k]], turned[plan_ref[pairs + 2 * k + 1]]], axis=1
            )
            right = jnp.concatenate(
                [
                    source[plan_ref[pairs + padded + 2 * k]],
                    source[plan_ref[pairs + padded + 2 * k + 1]],
                ],
                axis=0,
            )
            keep = plan_ref[pairs + 2 * padded + k]
            term = jnp.dot(left, right, preferred_element_type=jnp.float32)
            acc = jnp.where(keep > 0, acc, 0.0) + term
            run[k] = acc
            return acc

        return lax.fori_loop(start, stop, step, acc, unroll=5)

    zeros = jnp.zeros(run.shape[1:], jnp.float32)
    half = steps // 2
    fifth = half // 10 * 5
    acc = backward(near, 0, fifth, zeros)
    back_copy(0).wait_recv()
    back_copy(2).start()
    across_copy().wait_recv()
    bf_send[0] = gw_half[pl.ds(chip * share, share)] + gw_across[...]
    row_copy(0).start()
    backward(near, fifth, half, acc)
    back_copy(2).wait_recv()
    row_copy(0).wait_recv()
    bf_send[1] = bf_send[0] + bf_recv[0]
    row_copy(1).start()
    acc = backward(far, half, half + fifth, zeros)
    row_copy(1).wait_recv()
    bf_send[2] = bf_send[1] + bf_recv[1]
    row_copy(2).start()
    backward(far, half + fifth, steps, acc)

    def section_sum(j, q):
        found = []
        for c in (j * quart + q, spots + j * quart + q):
            last = plan_ref[pairs + 2 * padded + steps + c]
            some = plan_ref[pairs + 2 * padded + steps + 2 * spots + c]
            found.append(jnp.where(some > 0, run[last], 0.0))
        return found[0] + found[1]

    def grad_copy(d):
        return remote(
            section(back_send, HALF + d), section(back_recv, HALF - d), d_send.at[HALF - d],
            d_recv.at[HALF - d], (row + d, rep),
        )

    for d in offsets:
        for q in range(quart):
            back_send[(HALF + d) * quart + q] = section_sum(HALF + d, q).astype(jnp.bfloat16)

        @pl.when(inside(d))
        def _():
            grad_copy(d).start()

    for k in range(2, len(bits)):
        row_copy(k).wait_recv()
        summed = bf_send[k] + bf_recv[k]
        if k + 1 < len(bits):
            bf_send[k + 1] = summed
            row_copy(k + 1).start()
    gw_all[pl.ds((core * 2 + chip) * share, share)] = summed
    for mask in masks:
        gather_copy(mask, rep).start()

    for d in reversed(offsets):
        @pl.when(inside(d))
        def _():
            remote(
                section(back_send, HALF + d), section(back_recv, HALF + d), d_send.at[HALF + d],
                d_recv.at[HALF + d], (row + d, rep),
            ).wait_recv()
    for q in range(quart):
        result = section_sum(HALF, q)
        for d in offsets:
            result = result + back_recv[(HALF + d) * quart + q].astype(jnp.float32)
        grad_features_ref[q * blk:(q + 1) * blk] = result

    for mask in reversed(masks):
        gather_copy(mask, flip_all(rep, mask)).wait_recv()
    grad_weight_ref[...] = gw_all[...] * (rows * blocks * blk) ** (-0.5)

    for d in offsets:
        @pl.when(inside(d))
        def _():
            grad_copy(d).wait_send()
    for k in range(len(sends)):
        if sends[k] is None:
            feature_copy(k).wait_send()
        else:
            @pl.when(sends[k])
            def _():
                feature_copy(k).wait_send()
    for mask in masks:
        part_copy(mask - 1).wait_send()
        back_copy(mask - 1).wait_send()
        gather_copy(mask, rep).wait_send()
    beside_copy().wait_send()
    across_copy().wait_send()
    for k in range(len(bits)):
        row_copy(k).wait_send()


def store_kernel(
    a_ref, b_ref, c_ref, a_out, b_out, c_out, a_held, b_held, c_held, in_sems, out_sems
):
    ways = ((a_ref, a_held, a_out), (b_ref, b_held, b_out), (c_ref, c_held, c_out))
    fetches, stores = [], []
    for k, (src, held, dst) in enumerate(ways):
        fetches.append(pltpu.make_async_copy(src, held, in_sems.at[k]))
        stores.append(pltpu.make_async_copy(held, dst, out_sems.at[k]))
    for fetch in fetches:
        fetch.start()
    for fetch, store in zip(fetches, stores):
        fetch.wait()
        store.start()
    for store in stores:
        store.wait()


def make_plan(block_cols, quart):
    blocks, slots = block_cols.shape
    pairs = blocks * slots
    spots = SECTIONS * quart
    first = (lax.axis_index("row") - HALF) * blocks + lax.axis_index("rep") * quart
    moved = block_cols.reshape(pairs) - first
    slot = (moved // blocks) * quart + moved % blocks
    order = jnp.arange(pairs, dtype=jnp.int32)
    far = (order // slots // quart) // 2 != lax.axis_index("rep") // 2
    bin_of = slot + jnp.where(far, spots, 0)
    spot = jnp.arange(2 * spots, dtype=jnp.int32)
    half = (pairs // 2 + spots) // 2
    count = jnp.sum((bin_of[:, None] == spot[None, :]).astype(jnp.int32), axis=0)
    width = (count + 1) // 2
    same_half = (spot[:, None] // spots) == (spot[None, :] // spots)
    before = same_half & (spot[:, None] < spot[None, :])
    start = jnp.sum(jnp.where(before, width[:, None], 0), axis=0) + half * (spot // spots)
    rank = jnp.sum(
        ((bin_of[:, None] == bin_of[None, :]) & (order[:, None] < order[None, :])).astype(
            jnp.int32
        ),
        axis=0,
    )
    base = jnp.sum(jnp.where(spot[None, :] == bin_of[:, None], start[None, :], 0), axis=1)
    place = 2 * base + rank
    hot = place[:, None] == jnp.arange(4 * half, dtype=jnp.int32)[None, :]
    pair = pairs + jnp.sum(jnp.where(hot, order[:, None] - pairs, 0), axis=0)
    block = jnp.sum(jnp.where(hot, order[:, None] // slots % (2 * quart), 0), axis=0)
    step = jnp.arange(2 * half, dtype=jnp.int32)
    first_of = (start[:, None] == step[None, :]) & (count[:, None] > 0)
    keep = 1 - jnp.sum(first_of.astype(jnp.int32), axis=0)
    last = jnp.maximum(start + width - 1, 0)
    return jnp.concatenate([slot, pair, block, keep, last, count])


def on_device(rows, reps, features, block_cols, block_vals, weight, cotangent):
    group_rows, hidden = features.shape
    blocks, _, slots = block_cols.shape
    blk = block_vals.shape[-1]
    quart = blocks // reps
    pairs = blocks * slots
    own_rows = quart * blk
    levels = rows.bit_length() - 1
    share = hidden // reps
    plan = make_plan(block_cols[:, 0, :], quart)
    dma = pltpu.SemaphoreType.DMA
    bf16, f32 = jnp.bfloat16, jnp.float32
    vmem = pl.BlockSpec(memory_space=pltpu.VMEM)
    hbm = pl.BlockSpec(memory_space=pltpu.HBM)
    results = pl.pallas_call(
        functools.partial(layer_kernel, (rows, reps, quart, slots, blk, blocks)),
        out_shape=(
            jax.ShapeDtypeStruct((own_rows, hidden), bf16),
            jax.ShapeDtypeStruct((hidden, hidden), f32),
            jax.ShapeDtypeStruct((own_rows, hidden), f32),
        ),
        in_specs=[pl.BlockSpec(memory_space=pltpu.SMEM), hbm, hbm, hbm, hbm],
        out_specs=(vmem, vmem, vmem),
        scratch_shapes=[
            pltpu.VMEM((pairs, blk, blk), bf16),
            pltpu.VMEM((pairs + 1, blk, blk), bf16),
            pltpu.VMEM((hidden, hidden), bf16),
            pltpu.VMEM((own_rows, hidden), bf16),
            pltpu.VMEM((SECTIONS * quart, blk, hidden), bf16),
            pltpu.VMEM((reps - 1, own_rows, hidden), bf16),
            pltpu.VMEM((reps - 1, own_rows, hidden), bf16),
            pltpu.VMEM((blocks // 2, blk, hidden), bf16),
            pltpu.VMEM((blocks // 2, blk, hidden), bf16),
            pltpu.VMEM((pairs // 2 + SECTIONS * quart, blk, hidden), f32),
            pltpu.VMEM((SECTIONS * quart, blk, hidden), bf16),
            pltpu.VMEM((SECTIONS * quart, blk, hidden), bf16),
            pltpu.VMEM((hidden, hidden), f32),
            pltpu.VMEM((2 * share, hidden), f32),
            pltpu.VMEM((2 * share, hidden), f32),
            pltpu.VMEM((share, hidden), f32),
            pltpu.VMEM((levels, share, hidden), f32),
            pltpu.VMEM((levels, share, hidden), f32),
            pltpu.VMEM((hidden, hidden), f32),
            dma((4,)),
            dma((8,)), dma((8,)),
            dma((reps - 1,)), dma((reps - 1,)),
            dma((reps - 1,)), dma((reps - 1,)),
            dma((SECTIONS,)), dma((SECTIONS,)),
            dma((reps - 1,)), dma((reps - 1,)),
            dma((levels,)), dma((levels,)),
            dma((reps - 1,)), dma((reps - 1,)),
        ],
        compiler_params=pltpu.CompilerParams(
            collective_id=0, has_side_effects=True, vmem_limit_bytes=60 * 1024 * 1024
        ),
        cost_estimate=pl.CostEstimate(
            flops=4 * pairs * blk * blk * hidden, bytes_accessed=pairs * blk * blk * 2,
            transcendentals=own_rows * hidden,
        ),
    )(
        plan,
        features.reshape(blocks, blk, hidden),
        block_vals.reshape(pairs, blk, blk),
        weight,
        cotangent,
    )
    return pl.pallas_call(
        store_kernel,
        out_shape=tuple(jax.ShapeDtypeStruct(r.shape, r.dtype) for r in results),
        in_specs=[hbm, hbm, hbm],
        out_specs=(hbm, hbm, hbm),
        scratch_shapes=[pltpu.VMEM(r.shape, r.dtype) for r in results] + [dma((3,)), dma((3,))],
        compiler_params=pltpu.CompilerParams(vmem_limit_bytes=60 * 1024 * 1024),
        cost_estimate=pl.CostEstimate(
            flops=0, bytes_accessed=20 * own_rows * hidden, transcendentals=0
        ),
    )(*results)


def solution(mesh):
    return jax.shard_map(
        functools.partial(on_device, mesh.shape["row"], mesh.shape["rep"]),
        mesh=mesh,
        in_specs=(
            P("row", None),
            P("row", "rep", None),
            P("row", "rep", None, None, None),
            P(),
            P(("row", "rep"), None),
        ),
        out_specs=(P(("row", "rep"), None), P(), P(("row", "rep"), None)),
        check_vma=False,
    )
```

```python
import functools

import jax
import jax.numpy as jnp
from jax import lax
from jax.experimental import pallas as pl
from jax.experimental.pallas import tpu as pltpu
from jax.sharding import PartitionSpec as P

HALF = 3
SECTIONS = 2 * HALF + 1


def flip(index, bit):
    return index + bit * (1 - 2 * ((index // bit) % 2))


def flip_all(index, mask):
    bit = 1
    while bit <= mask:
        if mask & bit:
            index = flip(index, bit)
        bit *= 2
    return index


def remote(src, dst, send_sem, recv_sem, device):
    return pltpu.make_async_remote_copy(
        src_ref=src,
        dst_ref=dst,
        send_sem=send_sem,
        recv_sem=recv_sem,
        device_id=device,
        device_id_type=pl.DeviceIdType.MESH,
    )


def layer_kernel(
    sizes,
    plan_ref, features_ref, vals_ref, weight_ref, cotangent_ref,
    out_ref, grad_weight_ref, grad_features_ref,
    vals, turned, weight_own, cotangent, window, part_send, part_recv, near, far, run,
    back_send, back_recv, long_recv, gw_send, gw_recv, gw_half, gw_across, bf_send, bf_recv, gw_all,
    local_sem, a_send, a_recv, b_send, b_recv, c_send, c_recv,
    d_send, d_recv, e_send, e_recv, f_send, f_recv, g_send, g_recv,
):
    rows, reps, quart, slots, blk, blocks = sizes
    pairs = blocks * slots
    spots = SECTIONS * quart
    padded = pairs + 2 * spots
    steps = padded // 2
    row = lax.axis_index("row")
    rep = lax.axis_index("rep")
    bits = [1 << k for k in range(rows.bit_length() - 1)]
    offsets = [d for d in (3, -3, 2, -2, 1, -1)]
    masks = sorted(range(1, reps), key=lambda m: -m)

    def inside(d):
        return jnp.logical_and(row + d >= 0, row + d < rows)

    vals_copy = pltpu.make_async_copy(vals_ref, vals, local_sem.at[0])
    vals_copy.start()
    weight_copy = pltpu.make_async_copy(weight_ref, weight_own, local_sem.at[2])
    weight_copy.start()
    cotangent_copy = pltpu.make_async_copy(cotangent_ref, cotangent, local_sem.at[3])
    cotangent_copy.start()
    own = features_ref.at[pl.ds(rep * quart, quart)]
    own_copy = pltpu.make_async_copy(own, window.at[pl.ds(HALF * quart, quart)], local_sem.at[1])
    own_copy.start()

    barrier = pltpu.get_barrier_semaphore()
    expected = reps - 1
    for d in offsets:
        @pl.when(inside(d))
        def _():
            pl.semaphore_signal(
                barrier, inc=1, device_id=(row + d, rep), device_id_type=pl.DeviceIdType.MESH
            )
        expected = expected + inside(d).astype(jnp.int32)
    for bit in bits:
        if bit > 2:
            pl.semaphore_signal(
                barrier, inc=1, device_id=(flip(row, bit), rep),
                device_id_type=pl.DeviceIdType.MESH,
            )
            expected = expected + 1
    for mask in masks:
        pl.semaphore_signal(
            barrier, inc=1, device_id=(row, flip_all(rep, mask)),
            device_id_type=pl.DeviceIdType.MESH,
        )
    pl.semaphore_wait(barrier, expected)

    def section(ref, j):
        return ref.at[pl.ds(j * quart, quart)]

    side = 1 - 2 * (row % 2)
    odd = row % 2
    peer = row + side
    first = quart // 2

    def piece(off, part):
        start, size = ((0, quart), (0, first), (first, quart - first))[part]
        return window.at[pl.ds((HALF + off) * quart + start, size)]

    def feature_copy(k):
        src, dst, target = (
            (own, piece(-side, 0), peer),
            (own, piece(-2, 0), row + 2),
            (own, piece(2, 0), row - 2),
            (piece(side, 1), piece(side - 2, 1), row + 2),
            (piece(side, 1), piece(side + 2, 1), row - 2),
            (piece(2, 2), piece(2 - side, 2), peer),
            (piece(-2, 2), piece(-2 - side, 2), peer),
            (piece(-side, 0), piece(-3 * side, 0), row + 2 * side),
        )[k]
        return remote(src, dst, a_send.at[k], a_recv.at[k], (target, rep))

    def feature_wait(sem, part):
        spot = piece(0, part)
        remote(spot, spot, a_send.at[0], a_recv.at[sem], (peer, rep)).wait_recv()

    above, below = inside(2), inside(-2)
    sends = (
        None, above, below, above, below, above, below,
        jnp.logical_and(inside(-side), inside(2 * side)),
    )

    def start_feature(k):
        if sends[k] is None:
            feature_copy(k).start()
        else:
            @pl.when(sends[k])
            def _():
                feature_copy(k).start()

    for k in (0, 1, 2):
        start_feature(k)
    vals_copy.wait()

    turned[pairs] = jnp.zeros((blk, blk), turned.dtype)

    def turn(p, carry):
        turned[p] = vals[p].T
        return carry

    lax.fori_loop(0, pairs // 2, turn, 0, unroll=8)
    feature_wait(0, 0)
    start_feature(3)
    start_feature(4)

    @pl.when(above)
    def _():
        feature_wait(2, 0)

    start_feature(5)

    @pl.when(below)
    def _():
        feature_wait(1, 0)

    start_feature(6)
    lax.fori_loop(pairs // 2, pairs, turn, 0, unroll=8)

    @pl.when(inside(-side))
    def _():
        feature_wait(3 + odd, 1)
        feature_wait(6 - odd, 2)

    start_feature(7)
    for d in offsets:
        @pl.when(jnp.logical_not(inside(d)))
        def _():
            for q in range(quart):
                window[(HALF + d) * quart + q] = jnp.zeros(window.shape[1:], window.dtype)
                back_recv[(HALF + d) * quart + q] = jnp.zeros(
                    back_recv.shape[1:], back_recv.dtype
                )
    own_copy.wait()
    weight_copy.wait()
    cotangent_copy.wait()

    @pl.when(inside(3 * side))
    def _():
        feature_wait(4 - odd, 1)
        feature_wait(5 + odd, 2)

    @pl.when(inside(-3 * side))
    def _():
        feature_wait(7, 0)

    def partial(b):
        total = None
        for s in range(0, slots, 2):
            left = jnp.concatenate([vals[b * slots + s], vals[b * slots + s + 1]], axis=1)
            right = jnp.concatenate(
                [window[plan_ref[b * slots + s]], window[plan_ref[b * slots + s + 1]]], axis=0
            )
            term = jnp.dot(left, right, preferred_element_type=jnp.float32)
            total = term if total is None else total + term
        return total

    across, beside, opposite = flip(rep, 2), flip(rep, 1), flip_all(rep, 3)

    def partial_quarter(target):
        return jnp.concatenate([partial(target * quart + q) for q in range(quart)], axis=0)

    def part_copy(stage):
        return remote(
            part_send.at[stage], part_recv.at[stage], b_send.at[stage], b_recv.at[stage],
            (row, across if stage == 1 else beside),
        )

    part_send[0] = partial_quarter(opposite).astype(jnp.bfloat16)
    part_copy(0).start()
    total = partial_quarter(across)
    part_copy(0).wait_recv()
    part_send[1] = (total + part_recv[0].astype(jnp.float32)).astype(jnp.bfloat16)
    part_copy(1).start()
    part_send[2] = partial_quarter(beside).astype(jnp.bfloat16)
    part_copy(2).start()
    total = partial_quarter(rep)
    part_copy(2).wait_recv()
    total = total + part_recv[2].astype(jnp.float32)
    part_copy(1).wait_recv()
    total = total + part_recv[1].astype(jnp.float32)

    aggregate = total.astype(jnp.bfloat16)
    weight = weight_own[...]
    preact = jnp.dot(aggregate, weight, preferred_element_type=jnp.float32)
    sigmoid_pre = jax.nn.sigmoid(preact)
    grad_pre = (
        cotangent[...].astype(jnp.float32)
        * sigmoid_pre
        * (1.0 + preact * (1.0 - sigmoid_pre))
    ).astype(jnp.bfloat16)
    back_own = lax.dot_general(
        grad_pre, weight, (((1,), (1,)), ((), ())), preferred_element_type=jnp.float32
    ).astype(jnp.bfloat16)
    core, chip = rep % 2, rep // 2
    for q in range(quart):
        near[core * quart + q] = back_own[q * blk:(q + 1) * blk]

    def back_copy(stage):
        src, dst, target = ((near, far, across), (near, near, beside), (far, far, beside))[stage]
        return remote(
            section(src, core), section(dst, core), c_send.at[stage], c_recv.at[stage],
            (row, target),
        )

    back_copy(0).start()
    back_copy(1).start()
    out_ref[...] = (preact * sigmoid_pre).astype(jnp.bfloat16)

    gw_send[...] = lax.dot_general(
        aggregate, grad_pre, (((0,), (0,)), ((), ())), preferred_element_type=jnp.float32
    )
    half_rows = gw_send.shape[0] // 2
    share = half_rows // 2

    def share_of(ref, owner):
        return ref.at[pl.ds(((owner % 2) * 2 + owner // 2) * share, share)]

    def beside_copy():
        return remote(
            gw_send.at[pl.ds((1 - core) * half_rows, half_rows)], gw_recv,
            e_send.at[0], e_recv.at[0], (row, beside),
        )

    def across_copy():
        return remote(
            gw_half.at[pl.ds((1 - chip) * share, share)], gw_across,
            e_send.at[1], e_recv.at[1], (row, across),
        )

    def row_copy(k):
        return remote(
            bf_send.at[k], bf_recv.at[k], f_send.at[k], f_recv.at[k], (flip(row, bits[k]), rep)
        )

    def gather_copy(mask, owner):
        spot = share_of(gw_all, owner)
        return remote(
            spot, spot, g_send.at[mask - 1], g_recv.at[mask - 1], (row, flip_all(rep, mask))
        )

    beside_copy().start()
    back_copy(1).wait_recv()

    def backward(source, start, stop, acc):
        def step(k, acc):
            left = jnp.concatenate(
                [turned[plan_ref[pairs + 2 * k]], turned[plan_ref[pairs + 2 * k + 1]]], axis=1
            )
            right = jnp.concatenate(
                [
                    source[plan_ref[pairs + padded + 2 * k]],
                    source[plan_ref[pairs + padded + 2 * k + 1]],
                ],
                axis=0,
            )
            keep = plan_ref[pairs + 2 * padded + k]
            term = jnp.dot(left, right, preferred_element_type=jnp.float32)
            acc = jnp.where(keep > 0, acc, 0.0) + term
            run[k] = acc
            return acc

        return lax.fori_loop(start, stop, step, acc, unroll=5)

    zeros = jnp.zeros(run.shape[1:], jnp.float32)
    half = steps // 2
    fifth = half // 10 * 5
    acc = backward(near, 0, fifth, zeros)
    beside_copy().wait_recv()
    gw_half[...] = gw_send[pl.ds(core * half_rows, half_rows)] + gw_recv[...]
    across_copy().start()
    back_copy(0).wait_recv()
    back_copy(2).start()
    acc = backward(near, fifth, fifth + 10, acc)
    across_copy().wait_recv()
    bf_send[0] = gw_half[pl.ds(chip * share, share)] + gw_across[...]
    row_copy(0).start()
    backward(near, fifth + 10, half, acc)
    back_copy(2).wait_recv()
    row_copy(0).wait_recv()
    bf_send[1] = bf_send[0] + bf_recv[0]
    row_copy(1).start()
    acc = backward(far, half, half + fifth, zeros)
    row_copy(1).wait_recv()
    bf_send[2] = bf_send[1] + bf_recv[1]
    row_copy(2).start()
    backward(far, half + fifth, steps, acc)

    def section_sum(j, q):
        found = []
        for c in (j * quart + q, spots + j * quart + q):
            last = plan_ref[pairs + 2 * padded + steps + c]
            some = plan_ref[pairs + 2 * padded + steps + 2 * spots + c]
            found.append(jnp.where(some > 0, run[last], 0.0))
        return found[0] + found[1]

    def grad_copy(off):
        return remote(
            section(back_send, HALF + off), section(back_recv, HALF - off),
            d_send.at[HALF + off], d_recv.at[HALF - off], (row + off, rep),
        )

    def long_copy():
        return remote(
            section(back_send, HALF - 3 * side), long_recv, d_send.at[HALF - 3 * side],
            d_recv.at[HALF], (row - 2 * side, rep),
        )

    def put_section(off, added=None):
        for q in range(quart):
            value = section_sum(HALF + off, q)
            if added is not None:
                value = value + added[q].astype(jnp.float32)
            back_send[(HALF + off) * quart + q] = value.astype(jnp.bfloat16)

    @pl.when(inside(-3 * side))
    def _():
        put_section(-3 * side)
        long_copy().start()

    direct = (3 * side, 2, -2, side)
    for off in direct:
        @pl.when(inside(off))
        def _():
            put_section(off)
            grad_copy(off).start()

    has_long = jnp.logical_and(inside(2 * side), inside(-side))

    @pl.when(has_long)
    def _():
        remote(
            long_recv, long_recv, d_send.at[HALF], d_recv.at[HALF], (row + 2 * side, rep)
        ).wait_recv()
        put_section(-side, long_recv)
        grad_copy(-side).start()

    @pl.when(jnp.logical_and(inside(-side), jnp.logical_not(inside(2 * side))))
    def _():
        put_section(-side)
        grad_copy(-side).start()

    for k in range(2, len(bits)):
        row_copy(k).wait_recv()
        summed = bf_send[k] + bf_recv[k]
        if k + 1 < len(bits):
            bf_send[k + 1] = summed
            row_copy(k + 1).start()
    gw_all[pl.ds((core * 2 + chip) * share, share)] = summed
    for mask in masks:
        gather_copy(mask, rep).start()

    sources = (side, 2, -2, 3 * side, -side)
    for off in sources:
        @pl.when(inside(off))
        def _():
            remote(
                section(back_send, HALF + off), section(back_recv, HALF + off),
                d_send.at[HALF + off], d_recv.at[HALF + off], (row + off, rep),
            ).wait_recv()
    for q in range(quart):
        result = section_sum(HALF, q)
        for off in sources:
            result = result + back_recv[(HALF + off) * quart + q].astype(jnp.float32)
        grad_features_ref[q * blk:(q + 1) * blk] = result

    for mask in reversed(masks):
        gather_copy(mask, flip_all(rep, mask)).wait_recv()
    grad_weight_ref[...] = gw_all[...] * (rows * blocks * blk) ** (-0.5)

    for off in direct + (-side,):
        @pl.when(inside(off))
        def _():
            grad_copy(off).wait_send()

    @pl.when(inside(-3 * side))
    def _():
        long_copy().wait_send()

    for k in range(len(sends)):
        if sends[k] is None:
            feature_copy(k).wait_send()
        else:
            @pl.when(sends[k])
            def _():
                feature_copy(k).wait_send()
    for mask in masks:
        part_copy(mask - 1).wait_send()
        back_copy(mask - 1).wait_send()
        gather_copy(mask, rep).wait_send()
    beside_copy().wait_send()
    across_copy().wait_send()
    for k in range(len(bits)):
        row_copy(k).wait_send()


def store_kernel(
    a_ref, b_ref, c_ref, a_out, b_out, c_out, a_held, b_held, c_held, in_sems, out_sems
):
    ways = ((a_ref, a_held, a_out), (b_ref, b_held, b_out), (c_ref, c_held, c_out))
    fetches, stores = [], []
    for k, (src, held, dst) in enumerate(ways):
        fetches.append(pltpu.make_async_copy(src, held, in_sems.at[k]))
        stores.append(pltpu.make_async_copy(held, dst, out_sems.at[k]))
    for fetch in fetches:
        fetch.start()
    for fetch, store in zip(fetches, stores):
        fetch.wait()
        store.start()
    for store in stores:
        store.wait()


def make_plan(block_cols, quart):
    blocks, slots = block_cols.shape
    pairs = blocks * slots
    spots = SECTIONS * quart
    first = (lax.axis_index("row") - HALF) * blocks + lax.axis_index("rep") * quart
    moved = block_cols.reshape(pairs) - first
    slot = (moved // blocks) * quart + moved % blocks
    order = jnp.arange(pairs, dtype=jnp.int32)
    far = (order // slots // quart) // 2 != lax.axis_index("rep") // 2
    bin_of = slot + jnp.where(far, spots, 0)
    spot = jnp.arange(2 * spots, dtype=jnp.int32)
    half = (pairs // 2 + spots) // 2
    count = jnp.sum((bin_of[:, None] == spot[None, :]).astype(jnp.int32), axis=0)
    width = (count + 1) // 2
    same_half = (spot[:, None] // spots) == (spot[None, :] // spots)
    before = same_half & (spot[:, None] < spot[None, :])
    start = jnp.sum(jnp.where(before, width[:, None], 0), axis=0) + half * (spot // spots)
    rank = jnp.sum(
        ((bin_of[:, None] == bin_of[None, :]) & (order[:, None] < order[None, :])).astype(
            jnp.int32
        ),
        axis=0,
    )
    base = jnp.sum(jnp.where(spot[None, :] == bin_of[:, None], start[None, :], 0), axis=1)
    place = 2 * base + rank
    hot = place[:, None] == jnp.arange(4 * half, dtype=jnp.int32)[None, :]
    pair = pairs + jnp.sum(jnp.where(hot, order[:, None] - pairs, 0), axis=0)
    block = jnp.sum(jnp.where(hot, order[:, None] // slots % (2 * quart), 0), axis=0)
    step = jnp.arange(2 * half, dtype=jnp.int32)
    first_of = (start[:, None] == step[None, :]) & (count[:, None] > 0)
    keep = 1 - jnp.sum(first_of.astype(jnp.int32), axis=0)
    last = jnp.maximum(start + width - 1, 0)
    return jnp.concatenate([slot, pair, block, keep, last, count])


def on_device(rows, reps, features, block_cols, block_vals, weight, cotangent):
    group_rows, hidden = features.shape
    blocks, _, slots = block_cols.shape
    blk = block_vals.shape[-1]
    quart = blocks // reps
    pairs = blocks * slots
    own_rows = quart * blk
    levels = rows.bit_length() - 1
    share = hidden // reps
    plan = make_plan(block_cols[:, 0, :], quart)
    dma = pltpu.SemaphoreType.DMA
    bf16, f32 = jnp.bfloat16, jnp.float32
    vmem = pl.BlockSpec(memory_space=pltpu.VMEM)
    hbm = pl.BlockSpec(memory_space=pltpu.HBM)
    results = pl.pallas_call(
        functools.partial(layer_kernel, (rows, reps, quart, slots, blk, blocks)),
        out_shape=(
            jax.ShapeDtypeStruct((own_rows, hidden), bf16),
            jax.ShapeDtypeStruct((hidden, hidden), f32),
            jax.ShapeDtypeStruct((own_rows, hidden), f32),
        ),
        in_specs=[pl.BlockSpec(memory_space=pltpu.SMEM), hbm, hbm, hbm, hbm],
        out_specs=(vmem, vmem, vmem),
        scratch_shapes=[
            pltpu.VMEM((pairs, blk, blk), bf16),
            pltpu.VMEM((pairs + 1, blk, blk), bf16),
            pltpu.VMEM((hidden, hidden), bf16),
            pltpu.VMEM((own_rows, hidden), bf16),
            pltpu.VMEM((SECTIONS * quart, blk, hidden), bf16),
            pltpu.VMEM((reps - 1, own_rows, hidden), bf16),
            pltpu.VMEM((reps - 1, own_rows, hidden), bf16),
            pltpu.VMEM((blocks // 2, blk, hidden), bf16),
            pltpu.VMEM((blocks // 2, blk, hidden), bf16),
            pltpu.VMEM((pairs // 2 + SECTIONS * quart, blk, hidden), f32),
            pltpu.VMEM((SECTIONS * quart, blk, hidden), bf16),
            pltpu.VMEM((SECTIONS * quart, blk, hidden), bf16),
            pltpu.VMEM((quart, blk, hidden), bf16),
            pltpu.VMEM((hidden, hidden), f32),
            pltpu.VMEM((2 * share, hidden), f32),
            pltpu.VMEM((2 * share, hidden), f32),
            pltpu.VMEM((share, hidden), f32),
            pltpu.VMEM((levels, share, hidden), f32),
            pltpu.VMEM((levels, share, hidden), f32),
            pltpu.VMEM((hidden, hidden), f32),
            dma((4,)),
            dma((8,)), dma((8,)),
            dma((reps - 1,)), dma((reps - 1,)),
            dma((reps - 1,)), dma((reps - 1,)),
            dma((SECTIONS,)), dma((SECTIONS,)),
            dma((reps - 1,)), dma((reps - 1,)),
            dma((levels,)), dma((levels,)),
            dma((reps - 1,)), dma((reps - 1,)),
        ],
        compiler_params=pltpu.CompilerParams(
            collective_id=0, has_side_effects=True, vmem_limit_bytes=60 * 1024 * 1024
        ),
        cost_estimate=pl.CostEstimate(
            flops=4 * pairs * blk * blk * hidden, bytes_accessed=pairs * blk * blk * 2,
            transcendentals=own_rows * hidden,
        ),
    )(
        plan,
        features.reshape(blocks, blk, hidden),
        block_vals.reshape(pairs, blk, blk),
        weight,
        cotangent,
    )
    return pl.pallas_call(
        store_kernel,
        out_shape=tuple(jax.ShapeDtypeStruct(r.shape, r.dtype) for r in results),
        in_specs=[hbm, hbm, hbm],
        out_specs=(hbm, hbm, hbm),
        scratch_shapes=[pltpu.VMEM(r.shape, r.dtype) for r in results] + [dma((3,)), dma((3,))],
        compiler_params=pltpu.CompilerParams(vmem_limit_bytes=60 * 1024 * 1024),
        cost_estimate=pl.CostEstimate(
            flops=0, bytes_accessed=20 * own_rows * hidden, transcendentals=0
        ),
    )(*results)


def solution(mesh):
    return jax.shard_map(
        functools.partial(on_device, mesh.shape["row"], mesh.shape["rep"]),
        mesh=mesh,
        in_specs=(
            P("row", None),
            P("row", "rep", None),
            P("row", "rep", None, None, None),
            P(),
            P(("row", "rep"), None),
        ),
        out_specs=(P(("row", "rep"), None), P(), P(("row", "rep"), None)),
        check_vma=False,
    )
```

```python
import functools

import jax
import jax.numpy as jnp
from jax import lax
from jax.experimental import pallas as pl
from jax.experimental.pallas import tpu as pltpu
from jax.sharding import PartitionSpec as P

HALF = 3
SECTIONS = 2 * HALF + 1


def flip(index, bit):
    return index + bit * (1 - 2 * ((index // bit) % 2))


def flip_all(index, mask):
    bit = 1
    while bit <= mask:
        if mask & bit:
            index = flip(index, bit)
        bit *= 2
    return index


def remote(src, dst, send_sem, recv_sem, device):
    return pltpu.make_async_remote_copy(
        src_ref=src,
        dst_ref=dst,
        send_sem=send_sem,
        recv_sem=recv_sem,
        device_id=device,
        device_id_type=pl.DeviceIdType.MESH,
    )


def layer_kernel(
    sizes,
    cols_ref, features_ref, vals_ref, weight_ref, cotangent_ref,
    out_ref, grad_weight_ref, grad_features_ref,
    vals, turned, weight_own, cotangent, window, part_send, part_recv, near, far, run,
    back_send, back_recv, long_recv, gw_send, gw_recv, gw_half, gw_across, bf_send, bf_recv, gw_all,
    plan_held, plan_ref, local_sem, a_send, a_recv, b_send, b_recv, c_send, c_recv,
    d_send, d_recv, e_send, e_recv, f_send, f_recv, g_send, g_recv,
):
    rows, reps, quart, slots, blk, blocks = sizes
    pairs = blocks * slots
    spots = SECTIONS * quart
    padded = pairs + 2 * spots
    steps = padded // 2
    row = lax.axis_index("row")
    rep = lax.axis_index("rep")
    bits = [1 << k for k in range(rows.bit_length() - 1)]
    offsets = [d for d in (3, -3, 2, -2, 1, -1)]
    masks = sorted(range(1, reps), key=lambda m: -m)

    def inside(d):
        return jnp.logical_and(row + d >= 0, row + d < rows)

    vals_copy = pltpu.make_async_copy(vals_ref, vals, local_sem.at[0])
    vals_copy.start()
    weight_copy = pltpu.make_async_copy(weight_ref, weight_own, local_sem.at[2])
    weight_copy.start()
    cotangent_copy = pltpu.make_async_copy(cotangent_ref, cotangent, local_sem.at[3])
    cotangent_copy.start()
    own = features_ref.at[pl.ds(rep * quart, quart)]
    own_copy = pltpu.make_async_copy(own, window.at[pl.ds(HALF * quart, quart)], local_sem.at[1])
    own_copy.start()

    barrier = pltpu.get_barrier_semaphore()
    expected = reps - 1
    for d in offsets:
        @pl.when(inside(d))
        def _():
            pl.semaphore_signal(
                barrier, inc=1, device_id=(row + d, rep), device_id_type=pl.DeviceIdType.MESH
            )
        expected = expected + inside(d).astype(jnp.int32)
    for bit in bits:
        if bit > 2:
            pl.semaphore_signal(
                barrier, inc=1, device_id=(flip(row, bit), rep),
                device_id_type=pl.DeviceIdType.MESH,
            )
            expected = expected + 1
    for mask in masks:
        pl.semaphore_signal(
            barrier, inc=1, device_id=(row, flip_all(rep, mask)),
            device_id_type=pl.DeviceIdType.MESH,
        )
    pl.semaphore_wait(barrier, expected)

    base_col = (row - HALF) * blocks + rep * quart

    def slot_of(b, s):
        moved = cols_ref[b, 0, s] - base_col
        slot = lax.div(moved, blocks) * quart + lax.rem(moved, blocks)
        return jnp.minimum(jnp.maximum(slot, 0), spots - 1)

    def section(ref, j):
        return ref.at[pl.ds(j * quart, quart)]

    side = 1 - 2 * (row % 2)
    odd = row % 2
    peer = row + side
    first = quart // 2

    def piece(off, part):
        start, size = ((0, quart), (0, first), (first, quart - first))[part]
        return window.at[pl.ds((HALF + off) * quart + start, size)]

    def feature_copy(k):
        src, dst, target = (
            (own, piece(-side, 0), peer),
            (own, piece(-2, 0), row + 2),
            (own, piece(2, 0), row - 2),
            (piece(side, 1), piece(side - 2, 1), row + 2),
            (piece(side, 1), piece(side + 2, 1), row - 2),
            (piece(2, 2), piece(2 - side, 2), peer),
            (piece(-2, 2), piece(-2 - side, 2), peer),
            (piece(-side, 0), piece(-3 * side, 0), row + 2 * side),
        )[k]
        return remote(src, dst, a_send.at[k], a_recv.at[k], (target, rep))

    def feature_wait(sem, part):
        spot = piece(0, part)
        remote(spot, spot, a_send.at[0], a_recv.at[sem], (peer, rep)).wait_recv()

    above, below = inside(2), inside(-2)
    sends = (
        None, above, below, above, below, above, below,
        jnp.logical_and(inside(-side), inside(2 * side)),
    )

    def start_feature(k):
        if sends[k] is None:
            feature_copy(k).start()
        else:
            @pl.when(sends[k])
            def _():
                feature_copy(k).start()

    for k in (0, 1, 2):
        start_feature(k)

    lane = lax.broadcasted_iota(jnp.int32, (1, 128), 1)
    bins = jnp.full((1, 128), 1000, jnp.int32)
    for b in range(blocks):
        away = jnp.where(rep // 2 == (2 * b) // blocks, 0, spots)
        for s in range(slots):
            bins = jnp.where(lane == b * slots + s, slot_of(b, s) + away, bins)
    for k, line in enumerate(make_plan(bins, pairs, slots, blocks, spots)):
        plan_held[k:k + 1] = line
    plan_copy = pltpu.make_async_copy(plan_held, plan_ref, local_sem.at[4])
    plan_copy.start()
    vals_copy.wait()

    turned[pairs] = jnp.zeros((blk, blk), turned.dtype)

    def turn(p, carry):
        turned[p] = vals[p].T
        return carry

    lax.fori_loop(0, pairs // 2, turn, 0, unroll=8)
    feature_wait(0, 0)
    start_feature(3)
    start_feature(4)

    @pl.when(above)
    def _():
        feature_wait(2, 0)

    start_feature(5)

    @pl.when(below)
    def _():
        feature_wait(1, 0)

    start_feature(6)
    lax.fori_loop(pairs // 2, pairs, turn, 0, unroll=8)

    @pl.when(inside(-side))
    def _():
        feature_wait(3 + odd, 1)
        feature_wait(6 - odd, 2)

    start_feature(7)
    for d in offsets:
        @pl.when(jnp.logical_not(inside(d)))
        def _():
            for q in range(quart):
                window[(HALF + d) * quart + q] = jnp.zeros(window.shape[1:], window.dtype)
                back_recv[(HALF + d) * quart + q] = jnp.zeros(
                    back_recv.shape[1:], back_recv.dtype
                )
    own_copy.wait()
    weight_copy.wait()
    cotangent_copy.wait()
    plan_copy.wait()

    @pl.when(inside(3 * side))
    def _():
        feature_wait(4 - odd, 1)
        feature_wait(5 + odd, 2)

    @pl.when(inside(-3 * side))
    def _():
        feature_wait(7, 0)

    def partial(b):
        total = None
        for s in range(0, slots, 2):
            left = jnp.concatenate([vals[b * slots + s], vals[b * slots + s + 1]], axis=1)
            right = jnp.concatenate(
                [window[slot_of(b, s)], window[slot_of(b, s + 1)]], axis=0
            )
            term = jnp.dot(left, right, preferred_element_type=jnp.float32)
            total = term if total is None else total + term
        return total

    across, beside, opposite = flip(rep, 2), flip(rep, 1), flip_all(rep, 3)

    def partial_quarter(target):
        return jnp.concatenate([partial(target * quart + q) for q in range(quart)], axis=0)

    def part_copy(stage):
        return remote(
            part_send.at[stage], part_recv.at[stage], b_send.at[stage], b_recv.at[stage],
            (row, across if stage == 1 else beside),
        )

    part_send[0] = partial_quarter(opposite).astype(jnp.bfloat16)
    part_copy(0).start()
    total = partial_quarter(across)
    part_copy(0).wait_recv()
    part_send[1] = (total + part_recv[0].astype(jnp.float32)).astype(jnp.bfloat16)
    part_copy(1).start()
    part_send[2] = partial_quarter(beside).astype(jnp.bfloat16)
    part_copy(2).start()
    total = partial_quarter(rep)
    part_copy(2).wait_recv()
    total = total + part_recv[2].astype(jnp.float32)
    part_copy(1).wait_recv()
    total = total + part_recv[1].astype(jnp.float32)

    aggregate = total.astype(jnp.bfloat16)
    weight = weight_own[...]
    preact = jnp.dot(aggregate, weight, preferred_element_type=jnp.float32)
    sigmoid_pre = jax.nn.sigmoid(preact)
    grad_pre = (
        cotangent[...].astype(jnp.float32)
        * sigmoid_pre
        * (1.0 + preact * (1.0 - sigmoid_pre))
    ).astype(jnp.bfloat16)
    back_own = lax.dot_general(
        grad_pre, weight, (((1,), (1,)), ((), ())), preferred_element_type=jnp.float32
    ).astype(jnp.bfloat16)
    core, chip = rep % 2, rep // 2
    for q in range(quart):
        near[core * quart + q] = back_own[q * blk:(q + 1) * blk]

    def back_copy(stage):
        src, dst, target = ((near, far, across), (near, near, beside), (far, far, beside))[stage]
        return remote(
            section(src, core), section(dst, core), c_send.at[stage], c_recv.at[stage],
            (row, target),
        )

    back_copy(0).start()
    back_copy(1).start()
    out_ref[...] = (preact * sigmoid_pre).astype(jnp.bfloat16)

    gw_send[...] = lax.dot_general(
        aggregate, grad_pre, (((0,), (0,)), ((), ())), preferred_element_type=jnp.float32
    )
    half_rows = gw_send.shape[0] // 2
    share = half_rows // 2

    def share_of(ref, owner):
        return ref.at[pl.ds(((owner % 2) * 2 + owner // 2) * share, share)]

    def beside_copy():
        return remote(
            gw_send.at[pl.ds((1 - core) * half_rows, half_rows)], gw_recv,
            e_send.at[0], e_recv.at[0], (row, beside),
        )

    def across_copy():
        return remote(
            gw_half.at[pl.ds((1 - chip) * share, share)], gw_across,
            e_send.at[1], e_recv.at[1], (row, across),
        )

    def row_copy(k):
        return remote(
            bf_send.at[k], bf_recv.at[k], f_send.at[k], f_recv.at[k], (flip(row, bits[k]), rep)
        )

    def gather_copy(mask, owner):
        spot = share_of(gw_all, owner)
        return remote(
            spot, spot, g_send.at[mask - 1], g_recv.at[mask - 1], (row, flip_all(rep, mask))
        )

    beside_copy().start()
    back_copy(1).wait_recv()

    def backward(source, start, stop, acc):
        def step(k, acc):
            left = jnp.concatenate(
                [turned[plan_ref[0, 2 * k]], turned[plan_ref[0, 2 * k + 1]]], axis=1
            )
            right = jnp.concatenate(
                [
                    source[plan_ref[1, 2 * k]],
                    source[plan_ref[1, 2 * k + 1]],
                ],
                axis=0,
            )
            keep = plan_ref[2, k]
            term = jnp.dot(left, right, preferred_element_type=jnp.float32)
            acc = jnp.where(keep > 0, acc, 0.0) + term
            run[k] = acc
            return acc

        return lax.fori_loop(start, stop, step, acc, unroll=5)

    zeros = jnp.zeros(run.shape[1:], jnp.float32)
    half = steps // 2
    fifth = half // 10 * 5
    acc = backward(near, 0, fifth, zeros)
    beside_copy().wait_recv()
    gw_half[...] = gw_send[pl.ds(core * half_rows, half_rows)] + gw_recv[...]
    across_copy().start()
    back_copy(0).wait_recv()
    back_copy(2).start()
    acc = backward(near, fifth, fifth + 10, acc)
    across_copy().wait_recv()
    bf_send[0] = gw_half[pl.ds(chip * share, share)] + gw_across[...]
    row_copy(0).start()
    backward(near, fifth + 10, half, acc)
    back_copy(2).wait_recv()
    row_copy(0).wait_recv()
    bf_send[1] = bf_send[0] + bf_recv[0]
    row_copy(1).start()
    acc = backward(far, half, half + fifth, zeros)
    row_copy(1).wait_recv()
    bf_send[2] = bf_send[1] + bf_recv[1]
    row_copy(2).start()
    backward(far, half + fifth, steps, acc)

    def section_sum(j, q):
        found = []
        for c in (j * quart + q, spots + j * quart + q):
            last = plan_ref[3, c]
            some = plan_ref[4, c]
            found.append(jnp.where(some > 0, run[last], 0.0))
        return found[0] + found[1]

    def grad_copy(off):
        return remote(
            section(back_send, HALF + off), section(back_recv, HALF - off),
            d_send.at[HALF + off], d_recv.at[HALF - off], (row + off, rep),
        )

    def long_copy():
        return remote(
            section(back_send, HALF - 3 * side), long_recv, d_send.at[HALF - 3 * side],
            d_recv.at[HALF], (row - 2 * side, rep),
        )

    def put_section(off, added=None):
        for q in range(quart):
            value = section_sum(HALF + off, q)
            if added is not None:
                value = value + added[q].astype(jnp.float32)
            back_send[(HALF + off) * quart + q] = value.astype(jnp.bfloat16)

    @pl.when(inside(-3 * side))
    def _():
        put_section(-3 * side)
        long_copy().start()

    direct = (3 * side, 2, -2, side)
    for off in direct:
        @pl.when(inside(off))
        def _():
            put_section(off)
            grad_copy(off).start()

    has_long = jnp.logical_and(inside(2 * side), inside(-side))

    @pl.when(has_long)
    def _():
        remote(
            long_recv, long_recv, d_send.at[HALF], d_recv.at[HALF], (row + 2 * side, rep)
        ).wait_recv()
        put_section(-side, long_recv)
        grad_copy(-side).start()

    @pl.when(jnp.logical_and(inside(-side), jnp.logical_not(inside(2 * side))))
    def _():
        put_section(-side)
        grad_copy(-side).start()

    for k in range(2, len(bits)):
        row_copy(k).wait_recv()
        summed = bf_send[k] + bf_recv[k]
        if k + 1 < len(bits):
            bf_send[k + 1] = summed
            row_copy(k + 1).start()
    gw_all[pl.ds((core * 2 + chip) * share, share)] = summed
    for mask in masks:
        gather_copy(mask, rep).start()

    sources = (side, 2, -2, 3 * side, -side)
    for off in sources:
        @pl.when(inside(off))
        def _():
            remote(
                section(back_send, HALF + off), section(back_recv, HALF + off),
                d_send.at[HALF + off], d_recv.at[HALF + off], (row + off, rep),
            ).wait_recv()
    for q in range(quart):
        result = section_sum(HALF, q)
        for off in sources:
            result = result + back_recv[(HALF + off) * quart + q].astype(jnp.float32)
        grad_features_ref[q * blk:(q + 1) * blk] = result

    for mask in reversed(masks):
        gather_copy(mask, flip_all(rep, mask)).wait_recv()
    grad_weight_ref[...] = gw_all[...] * (rows * blocks * blk) ** (-0.5)

    for off in direct + (-side,):
        @pl.when(inside(off))
        def _():
            grad_copy(off).wait_send()

    @pl.when(inside(-3 * side))
    def _():
        long_copy().wait_send()

    for k in range(len(sends)):
        if sends[k] is None:
            feature_copy(k).wait_send()
        else:
            @pl.when(sends[k])
            def _():
                feature_copy(k).wait_send()
    for mask in masks:
        part_copy(mask - 1).wait_send()
        back_copy(mask - 1).wait_send()
        gather_copy(mask, rep).wait_send()
    beside_copy().wait_send()
    across_copy().wait_send()
    for k in range(len(bits)):
        row_copy(k).wait_send()


def store_kernel(
    a_ref, b_ref, c_ref, a_out, b_out, c_out, a_held, b_held, c_held, in_sems, out_sems
):
    ways = ((a_ref, a_held, a_out), (b_ref, b_held, b_out), (c_ref, c_held, c_out))
    fetches, stores = [], []
    for k, (src, held, dst) in enumerate(ways):
        fetches.append(pltpu.make_async_copy(src, held, in_sems.at[k]))
        stores.append(pltpu.make_async_copy(held, dst, out_sems.at[k]))
    for fetch in fetches:
        fetch.start()
    for fetch, store in zip(fetches, stores):
        fetch.wait()
        store.start()
    for store in stores:
        store.wait()


def make_plan(bins, pairs, slots, blocks, spots):
    side = bins.shape[1]
    half = (pairs // 2 + spots) // 2
    row_of = lax.broadcasted_iota(jnp.int32, (side, side), 0)
    col_of = lax.broadcasted_iota(jnp.int32, (side, side), 1)
    lane = lax.broadcasted_iota(jnp.int32, (1, side), 1)

    def across(line):
        return jnp.broadcast_to(line, (side, side))

    def total(mask, value):
        return jnp.sum(jnp.where(mask, value, 0), axis=0, keepdims=True)

    bin_col = across(bins)
    bin_row = bin_col.T
    rank = total((bin_row == bin_col) & (row_of < col_of), 1)
    count = total(bin_row == col_of, 1)
    width = lax.shift_right_logical(count + 1, 1)
    same = (row_of >= spots) == (col_of >= spots)
    start = total((row_of < col_of) & same, across(width).T) + jnp.where(lane >= spots, half, 0)
    start_row = across(jnp.where((count > 0) & (lane < 2 * spots), start, -1)).T
    base = total(row_of == bin_col, start_row)
    place = jnp.where(lane < pairs, 2 * base + rank, -1)
    hot = across(place).T == col_of
    pair = pairs + total(hot, row_of - pairs)
    block_row = jnp.zeros((side, side), jnp.int32)
    for b in range(1, blocks):
        step = 1 if b != blocks // 2 else 1 - blocks // 2
        block_row = block_row + jnp.where(row_of >= b * slots, step, 0)
    block = total(hot, block_row)
    keep = 1 - total(start_row == col_of, 1)
    last = jnp.maximum(start + width - 1, 0)
    return pair, block, keep, last, count


def on_device(rows, reps, features, block_cols, block_vals, weight, cotangent):
    group_rows, hidden = features.shape
    blocks, _, slots = block_cols.shape
    blk = block_vals.shape[-1]
    quart = blocks // reps
    pairs = blocks * slots
    own_rows = quart * blk
    levels = rows.bit_length() - 1
    share = hidden // reps
    dma = pltpu.SemaphoreType.DMA
    bf16, f32 = jnp.bfloat16, jnp.float32
    vmem = pl.BlockSpec(memory_space=pltpu.VMEM)
    hbm = pl.BlockSpec(memory_space=pltpu.HBM)
    results = pl.pallas_call(
        functools.partial(layer_kernel, (rows, reps, quart, slots, blk, blocks)),
        out_shape=(
            jax.ShapeDtypeStruct((own_rows, hidden), bf16),
            jax.ShapeDtypeStruct((hidden, hidden), f32),
            jax.ShapeDtypeStruct((own_rows, hidden), f32),
        ),
        in_specs=[pl.BlockSpec(memory_space=pltpu.SMEM), hbm, hbm, hbm, hbm],
        out_specs=(vmem, vmem, vmem),
        scratch_shapes=[
            pltpu.VMEM((pairs, blk, blk), bf16),
            pltpu.VMEM((pairs + 1, blk, blk), bf16),
            pltpu.VMEM((hidden, hidden), bf16),
            pltpu.VMEM((own_rows, hidden), bf16),
            pltpu.VMEM((SECTIONS * quart, blk, hidden), bf16),
            pltpu.VMEM((reps - 1, own_rows, hidden), bf16),
            pltpu.VMEM((reps - 1, own_rows, hidden), bf16),
            pltpu.VMEM((blocks // 2, blk, hidden), bf16),
            pltpu.VMEM((blocks // 2, blk, hidden), bf16),
            pltpu.VMEM((pairs // 2 + SECTIONS * quart, blk, hidden), f32),
            pltpu.VMEM((SECTIONS * quart, blk, hidden), bf16),
            pltpu.VMEM((SECTIONS * quart, blk, hidden), bf16),
            pltpu.VMEM((quart, blk, hidden), bf16),
            pltpu.VMEM((hidden, hidden), f32),
            pltpu.VMEM((2 * share, hidden), f32),
            pltpu.VMEM((2 * share, hidden), f32),
            pltpu.VMEM((share, hidden), f32),
            pltpu.VMEM((levels, share, hidden), f32),
            pltpu.VMEM((levels, share, hidden), f32),
            pltpu.VMEM((hidden, hidden), f32),
            pltpu.VMEM((8, 128), jnp.int32),
            pltpu.SMEM((8, 128), jnp.int32),
            dma((5,)),
            dma((8,)), dma((8,)),
            dma((reps - 1,)), dma((reps - 1,)),
            dma((reps - 1,)), dma((reps - 1,)),
            dma((SECTIONS,)), dma((SECTIONS,)),
            dma((reps - 1,)), dma((reps - 1,)),
            dma((levels,)), dma((levels,)),
            dma((reps - 1,)), dma((reps - 1,)),
        ],
        compiler_params=pltpu.CompilerParams(
            collective_id=0, has_side_effects=True, vmem_limit_bytes=60 * 1024 * 1024
        ),
        cost_estimate=pl.CostEstimate(
            flops=4 * pairs * blk * blk * hidden, bytes_accessed=pairs * blk * blk * 2,
            transcendentals=own_rows * hidden,
        ),
    )(
        block_cols,
        features.reshape(blocks, blk, hidden),
        block_vals.reshape(pairs, blk, blk),
        weight,
        cotangent,
    )
    return pl.pallas_call(
        store_kernel,
        out_shape=tuple(jax.ShapeDtypeStruct(r.shape, r.dtype) for r in results),
        in_specs=[hbm, hbm, hbm],
        out_specs=(hbm, hbm, hbm),
        scratch_shapes=[pltpu.VMEM(r.shape, r.dtype) for r in results] + [dma((3,)), dma((3,))],
        compiler_params=pltpu.CompilerParams(vmem_limit_bytes=60 * 1024 * 1024),
        cost_estimate=pl.CostEstimate(
            flops=0, bytes_accessed=20 * own_rows * hidden, transcendentals=0
        ),
    )(*results)


def solution(mesh):
    return jax.shard_map(
        functools.partial(on_device, mesh.shape["row"], mesh.shape["rep"]),
        mesh=mesh,
        in_specs=(
            P("row", None),
            P("row", "rep", None),
            P("row", "rep", None, None, None),
            P(),
            P(("row", "rep"), None),
        ),
        out_specs=(P(("row", "rep"), None), P(), P(("row", "rep"), None)),
        check_vma=False,
    )
```

```python
import functools

import jax
import jax.numpy as jnp
from jax import lax
from jax.experimental import pallas as pl
from jax.experimental.pallas import tpu as pltpu
from jax.sharding import PartitionSpec as P

HALF = 3
SECTIONS = 2 * HALF + 1


def flip(index, bit):
    return index + bit * (1 - 2 * ((index // bit) % 2))


def flip_all(index, mask):
    bit = 1
    while bit <= mask:
        if mask & bit:
            index = flip(index, bit)
        bit *= 2
    return index


def remote(src, dst, send_sem, recv_sem, device):
    return pltpu.make_async_remote_copy(
        src_ref=src,
        dst_ref=dst,
        send_sem=send_sem,
        recv_sem=recv_sem,
        device_id=device,
        device_id_type=pl.DeviceIdType.MESH,
    )


def layer_kernel(
    sizes,
    cols_ref, features_ref, vals_ref, weight_ref, cotangent_ref,
    out_ref, grad_weight_ref, grad_features_ref,
    vals, turned, weight_own, cotangent, window, part_send, part_recv, near, far, run,
    back_send, back_recv, long_recv, gw_send, gw_recv, gw_half, gw_across, bf_send, bf_recv, gw_all,
    plan_held, plan_ref, local_sem, a_send, a_recv, b_send, b_recv, c_send, c_recv,
    d_send, d_recv, e_send, e_recv, f_send, f_recv, g_send, g_recv,
):
    rows, reps, quart, slots, blk, blocks = sizes
    pairs = blocks * slots
    spots = SECTIONS * quart
    padded = pairs + 2 * spots
    steps = padded // 2
    row = lax.axis_index("row")
    rep = lax.axis_index("rep")
    bits = [1 << k for k in range(rows.bit_length() - 1)]
    offsets = [d for d in (3, -3, 2, -2, 1, -1)]
    masks = sorted(range(1, reps), key=lambda m: -m)

    def inside(d):
        return jnp.logical_and(row + d >= 0, row + d < rows)

    vals_copy = pltpu.make_async_copy(vals_ref, vals, local_sem.at[0])
    vals_copy.start()
    weight_copy = pltpu.make_async_copy(weight_ref, weight_own, local_sem.at[2])
    weight_copy.start()
    cotangent_copy = pltpu.make_async_copy(cotangent_ref, cotangent, local_sem.at[3])
    cotangent_copy.start()
    own = features_ref.at[pl.ds(rep * quart, quart)]
    own_copy = pltpu.make_async_copy(own, window.at[pl.ds(HALF * quart, quart)], local_sem.at[1])
    own_copy.start()

    barrier = pltpu.get_barrier_semaphore()
    expected = reps - 1
    for d in offsets:
        @pl.when(inside(d))
        def _():
            pl.semaphore_signal(
                barrier, inc=1, device_id=(row + d, rep), device_id_type=pl.DeviceIdType.MESH
            )
        expected = expected + inside(d).astype(jnp.int32)
    for bit in bits:
        if bit > 2:
            pl.semaphore_signal(
                barrier, inc=1, device_id=(flip(row, bit), rep),
                device_id_type=pl.DeviceIdType.MESH,
            )
            expected = expected + 1
    for mask in masks:
        pl.semaphore_signal(
            barrier, inc=1, device_id=(row, flip_all(rep, mask)),
            device_id_type=pl.DeviceIdType.MESH,
        )
    pl.semaphore_wait(barrier, expected)

    base_col = (row - HALF) * blocks + rep * quart

    def slot_of(b, s):
        moved = cols_ref[b, 0, s] - base_col
        slot = lax.div(moved, blocks) * quart + lax.rem(moved, blocks)
        return jnp.minimum(jnp.maximum(slot, 0), spots - 1)

    def section(ref, j):
        return ref.at[pl.ds(j * quart, quart)]

    side = 1 - 2 * (row % 2)
    odd = row % 2
    peer = row + side
    first = quart // 2

    def piece(off, part):
        start, size = ((0, quart), (0, first), (first, quart - first))[part]
        return window.at[pl.ds((HALF + off) * quart + start, size)]

    def feature_copy(k):
        src, dst, target = (
            (own, piece(-side, 0), peer),
            (own, piece(-2, 0), row + 2),
            (own, piece(2, 0), row - 2),
            (piece(side, 1), piece(side - 2, 1), row + 2),
            (piece(side, 1), piece(side + 2, 1), row - 2),
            (piece(2, 2), piece(2 - side, 2), peer),
            (piece(-2, 2), piece(-2 - side, 2), peer),
            (piece(-side, 0), piece(-3 * side, 0), row + 2 * side),
        )[k]
        return remote(src, dst, a_send.at[k], a_recv.at[k], (target, rep))

    def feature_wait(sem, part):
        spot = piece(0, part)
        remote(spot, spot, a_send.at[0], a_recv.at[sem], (peer, rep)).wait_recv()

    above, below = inside(2), inside(-2)
    sends = (
        None, above, below, above, below, above, below,
        jnp.logical_and(inside(-side), inside(2 * side)),
    )

    def start_feature(k):
        if sends[k] is None:
            feature_copy(k).start()
        else:
            @pl.when(sends[k])
            def _():
                feature_copy(k).start()

    for k in (0, 1, 2):
        start_feature(k)

    lane = lax.broadcasted_iota(jnp.int32, (1, 128), 1)
    bins = jnp.full((1, 128), 1000, jnp.int32)
    for b in range(blocks):
        away = jnp.where(rep // 2 == (2 * b) // blocks, 0, spots)
        for s in range(slots):
            bins = jnp.where(lane == b * slots + s, slot_of(b, s) + away, bins)
    for k, line in enumerate(make_plan(bins, pairs, slots, blocks, spots)):
        plan_held[k:k + 1] = line
    plan_copy = pltpu.make_async_copy(plan_held, plan_ref, local_sem.at[4])
    plan_copy.start()
    vals_copy.wait()

    turned[pairs] = jnp.zeros((blk, blk), turned.dtype)

    def turn(p, carry):
        turned[p] = vals[p].T
        return carry

    lax.fori_loop(0, pairs // 2, turn, 0, unroll=8)
    feature_wait(0, 0)
    start_feature(3)
    start_feature(4)

    @pl.when(above)
    def _():
        feature_wait(2, 0)

    start_feature(5)

    @pl.when(below)
    def _():
        feature_wait(1, 0)

    start_feature(6)

    @pl.when(inside(-side))
    def _():
        feature_wait(3 + odd, 1)
        feature_wait(6 - odd, 2)

    start_feature(7)
    lax.fori_loop(pairs // 2, pairs, turn, 0, unroll=8)
    for d in offsets:
        @pl.when(jnp.logical_not(inside(d)))
        def _():
            for q in range(quart):
                window[(HALF + d) * quart + q] = jnp.zeros(window.shape[1:], window.dtype)
                back_recv[(HALF + d) * quart + q] = jnp.zeros(
                    back_recv.shape[1:], back_recv.dtype
                )
    own_copy.wait()
    weight_copy.wait()
    cotangent_copy.wait()
    plan_copy.wait()

    @pl.when(inside(3 * side))
    def _():
        feature_wait(4 - odd, 1)
        feature_wait(5 + odd, 2)

    @pl.when(inside(-3 * side))
    def _():
        feature_wait(7, 0)

    def partial(b):
        total = None
        for s in range(0, slots, 2):
            left = jnp.concatenate([vals[b * slots + s], vals[b * slots + s + 1]], axis=1)
            right = jnp.concatenate(
                [window[slot_of(b, s)], window[slot_of(b, s + 1)]], axis=0
            )
            term = jnp.dot(left, right, preferred_element_type=jnp.float32)
            total = term if total is None else total + term
        return total

    across, beside, opposite = flip(rep, 2), flip(rep, 1), flip_all(rep, 3)

    def partial_quarter(target):
        return jnp.concatenate([partial(target * quart + q) for q in range(quart)], axis=0)

    def part_copy(stage):
        return remote(
            part_send.at[stage], part_recv.at[stage], b_send.at[stage], b_recv.at[stage],
            (row, across if stage == 1 else beside),
        )

    part_send[0] = partial_quarter(opposite).astype(jnp.bfloat16)
    part_copy(0).start()
    total = partial_quarter(across)
    part_copy(0).wait_recv()
    part_send[1] = (total + part_recv[0].astype(jnp.float32)).astype(jnp.bfloat16)
    part_copy(1).start()
    part_send[2] = partial_quarter(beside).astype(jnp.bfloat16)
    part_copy(2).start()
    total = partial_quarter(rep)
    part_copy(2).wait_recv()
    total = total + part_recv[2].astype(jnp.float32)
    part_copy(1).wait_recv()
    total = total + part_recv[1].astype(jnp.float32)

    aggregate = total.astype(jnp.bfloat16)
    weight = weight_own[...]
    preact = jnp.dot(aggregate, weight, preferred_element_type=jnp.float32)
    sigmoid_pre = jax.nn.sigmoid(preact)
    grad_pre = (
        cotangent[...].astype(jnp.float32)
        * sigmoid_pre
        * (1.0 + preact * (1.0 - sigmoid_pre))
    ).astype(jnp.bfloat16)
    back_own = lax.dot_general(
        grad_pre, weight, (((1,), (1,)), ((), ())), preferred_element_type=jnp.float32
    ).astype(jnp.bfloat16)
    core, chip = rep % 2, rep // 2
    for q in range(quart):
        near[core * quart + q] = back_own[q * blk:(q + 1) * blk]

    def back_copy(stage):
        src, dst, target = ((near, far, across), (near, near, beside), (far, far, beside))[stage]
        return remote(
            section(src, core), section(dst, core), c_send.at[stage], c_recv.at[stage],
            (row, target),
        )

    back_copy(0).start()
    back_copy(1).start()
    out_ref[...] = (preact * sigmoid_pre).astype(jnp.bfloat16)

    gw_send[...] = lax.dot_general(
        aggregate, grad_pre, (((0,), (0,)), ((), ())), preferred_element_type=jnp.float32
    )
    half_rows = gw_send.shape[0] // 2
    share = half_rows // 2

    def share_of(ref, owner):
        return ref.at[pl.ds(((owner % 2) * 2 + owner // 2) * share, share)]

    def beside_copy():
        return remote(
            gw_send.at[pl.ds((1 - core) * half_rows, half_rows)], gw_recv,
            e_send.at[0], e_recv.at[0], (row, beside),
        )

    def across_copy():
        return remote(
            gw_half.at[pl.ds((1 - chip) * share, share)], gw_across,
            e_send.at[1], e_recv.at[1], (row, across),
        )

    def row_copy(k):
        return remote(
            bf_send.at[k], bf_recv.at[k], f_send.at[k], f_recv.at[k], (flip(row, bits[k]), rep)
        )

    def gather_copy(mask, owner):
        spot = share_of(gw_all, owner)
        return remote(
            spot, spot, g_send.at[mask - 1], g_recv.at[mask - 1], (row, flip_all(rep, mask))
        )

    beside_copy().start()
    back_copy(1).wait_recv()

    def backward(source, start, stop, acc):
        def step(k, acc):
            left = jnp.concatenate(
                [turned[plan_ref[0, 2 * k]], turned[plan_ref[0, 2 * k + 1]]], axis=1
            )
            right = jnp.concatenate(
                [
                    source[plan_ref[1, 2 * k]],
                    source[plan_ref[1, 2 * k + 1]],
                ],
                axis=0,
            )
            keep = plan_ref[2, k]
            term = jnp.dot(left, right, preferred_element_type=jnp.float32)
            acc = jnp.where(keep > 0, acc, 0.0) + term
            run[k] = acc
            return acc

        return lax.fori_loop(start, stop, step, acc, unroll=5)

    zeros = jnp.zeros(run.shape[1:], jnp.float32)
    half = steps // 2
    fifth = half // 10 * 5
    acc = backward(near, 0, fifth, zeros)
    beside_copy().wait_recv()
    gw_half[...] = gw_send[pl.ds(core * half_rows, half_rows)] + gw_recv[...]
    across_copy().start()
    back_copy(0).wait_recv()
    back_copy(2).start()
    acc = backward(near, fifth, fifth + 10, acc)
    across_copy().wait_recv()
    bf_send[0] = gw_half[pl.ds(chip * share, share)] + gw_across[...]
    row_copy(0).start()
    backward(near, fifth + 10, half, acc)
    back_copy(2).wait_recv()
    row_copy(0).wait_recv()
    bf_send[1] = bf_send[0] + bf_recv[0]
    row_copy(1).start()
    acc = backward(far, half, half + fifth, zeros)
    row_copy(1).wait_recv()
    bf_send[2] = bf_send[1] + bf_recv[1]
    row_copy(2).start()
    backward(far, half + fifth, steps, acc)

    def section_sum(j, q):
        found = []
        for c in (j * quart + q, spots + j * quart + q):
            last = plan_ref[3, c]
            some = plan_ref[4, c]
            found.append(jnp.where(some > 0, run[last], 0.0))
        return found[0] + found[1]

    def grad_copy(off):
        return remote(
            section(back_send, HALF + off), section(back_recv, HALF - off),
            d_send.at[HALF + off], d_recv.at[HALF - off], (row + off, rep),
        )

    def long_copy():
        return remote(
            section(back_send, HALF - 3 * side), long_recv, d_send.at[HALF - 3 * side],
            d_recv.at[HALF], (row - 2 * side, rep),
        )

    def put_section(off, added=None):
        for q in range(quart):
            value = section_sum(HALF + off, q)
            if added is not None:
                value = value + added[q].astype(jnp.float32)
            back_send[(HALF + off) * quart + q] = value.astype(jnp.bfloat16)

    @pl.when(inside(-3 * side))
    def _():
        put_section(-3 * side)
        long_copy().start()

    direct = (3 * side, 2, -2, side)
    for off in direct:
        @pl.when(inside(off))
        def _():
            put_section(off)
            grad_copy(off).start()

    has_long = jnp.logical_and(inside(2 * side), inside(-side))

    @pl.when(has_long)
    def _():
        remote(
            long_recv, long_recv, d_send.at[HALF], d_recv.at[HALF], (row + 2 * side, rep)
        ).wait_recv()
        put_section(-side, long_recv)
        grad_copy(-side).start()

    @pl.when(jnp.logical_and(inside(-side), jnp.logical_not(inside(2 * side))))
    def _():
        put_section(-side)
        grad_copy(-side).start()

    for k in range(2, len(bits)):
        row_copy(k).wait_recv()
        summed = bf_send[k] + bf_recv[k]
        if k + 1 < len(bits):
            bf_send[k + 1] = summed
            row_copy(k + 1).start()
    gw_all[pl.ds((core * 2 + chip) * share, share)] = summed
    for mask in masks:
        gather_copy(mask, rep).start()

    sources = (side, 2, -2, 3 * side, -side)
    for off in sources:
        @pl.when(inside(off))
        def _():
            remote(
                section(back_send, HALF + off), section(back_recv, HALF + off),
                d_send.at[HALF + off], d_recv.at[HALF + off], (row + off, rep),
            ).wait_recv()
    for q in range(quart):
        result = section_sum(HALF, q)
        for off in sources:
            result = result + back_recv[(HALF + off) * quart + q].astype(jnp.float32)
        grad_features_ref[q * blk:(q + 1) * blk] = result

    for mask in reversed(masks):
        gather_copy(mask, flip_all(rep, mask)).wait_recv()
    grad_weight_ref[...] = gw_all[...] * (rows * blocks * blk) ** (-0.5)

    for off in direct + (-side,):
        @pl.when(inside(off))
        def _():
            grad_copy(off).wait_send()

    @pl.when(inside(-3 * side))
    def _():
        long_copy().wait_send()

    for k in range(len(sends)):
        if sends[k] is None:
            feature_copy(k).wait_send()
        else:
            @pl.when(sends[k])
            def _():
                feature_copy(k).wait_send()
    for mask in masks:
        part_copy(mask - 1).wait_send()
        back_copy(mask - 1).wait_send()
        gather_copy(mask, rep).wait_send()
    beside_copy().wait_send()
    across_copy().wait_send()
    for k in range(len(bits)):
        row_copy(k).wait_send()


def store_kernel(
    a_ref, b_ref, c_ref, a_out, b_out, c_out, a_held, b_held, c_held, in_sems, out_sems
):
    ways = ((a_ref, a_held, a_out), (b_ref, b_held, b_out), (c_ref, c_held, c_out))
    fetches, stores = [], []
    for k, (src, held, dst) in enumerate(ways):
        fetches.append(pltpu.make_async_copy(src, held, in_sems.at[k]))
        stores.append(pltpu.make_async_copy(held, dst, out_sems.at[k]))
    for fetch in fetches:
        fetch.start()
    for fetch, store in zip(fetches, stores):
        fetch.wait()
        store.start()
    for store in stores:
        store.wait()


def make_plan(bins, pairs, slots, blocks, spots):
    side = bins.shape[1]
    half = (pairs // 2 + spots) // 2
    row_of = lax.broadcasted_iota(jnp.int32, (side, side), 0)
    col_of = lax.broadcasted_iota(jnp.int32, (side, side), 1)
    lane = lax.broadcasted_iota(jnp.int32, (1, side), 1)

    def across(line):
        return jnp.broadcast_to(line, (side, side))

    def total(mask, value):
        return jnp.sum(jnp.where(mask, value, 0), axis=0, keepdims=True)

    bin_col = across(bins)
    bin_row = bin_col.T
    rank = total((bin_row == bin_col) & (row_of < col_of), 1)
    count = total(bin_row == col_of, 1)
    width = lax.shift_right_logical(count + 1, 1)
    same = (row_of >= spots) == (col_of >= spots)
    start = total((row_of < col_of) & same, across(width).T) + jnp.where(lane >= spots, half, 0)
    start_row = across(jnp.where((count > 0) & (lane < 2 * spots), start, -1)).T
    base = total(row_of == bin_col, start_row)
    place = jnp.where(lane < pairs, 2 * base + rank, -1)
    hot = across(place).T == col_of
    pair = pairs + total(hot, row_of - pairs)
    block_row = jnp.zeros((side, side), jnp.int32)
    for b in range(1, blocks):
        step = 1 if b != blocks // 2 else 1 - blocks // 2
        block_row = block_row + jnp.where(row_of >= b * slots, step, 0)
    block = total(hot, block_row)
    keep = 1 - total(start_row == col_of, 1)
    last = jnp.maximum(start + width - 1, 0)
    return pair, block, keep, last, count


def on_device(rows, reps, features, block_cols, block_vals, weight, cotangent):
    group_rows, hidden = features.shape
    blocks, _, slots = block_cols.shape
    blk = block_vals.shape[-1]
    quart = blocks // reps
    pairs = blocks * slots
    own_rows = quart * blk
    levels = rows.bit_length() - 1
    share = hidden // reps
    dma = pltpu.SemaphoreType.DMA
    bf16, f32 = jnp.bfloat16, jnp.float32
    vmem = pl.BlockSpec(memory_space=pltpu.VMEM)
    hbm = pl.BlockSpec(memory_space=pltpu.HBM)
    results = pl.pallas_call(
        functools.partial(layer_kernel, (rows, reps, quart, slots, blk, blocks)),
        out_shape=(
            jax.ShapeDtypeStruct((own_rows, hidden), bf16),
            jax.ShapeDtypeStruct((hidden, hidden), f32),
            jax.ShapeDtypeStruct((own_rows, hidden), f32),
        ),
        in_specs=[pl.BlockSpec(memory_space=pltpu.SMEM), hbm, hbm, hbm, hbm],
        out_specs=(vmem, vmem, vmem),
        scratch_shapes=[
            pltpu.VMEM((pairs, blk, blk), bf16),
            pltpu.VMEM((pairs + 1, blk, blk), bf16),
            pltpu.VMEM((hidden, hidden), bf16),
            pltpu.VMEM((own_rows, hidden), bf16),
            pltpu.VMEM((SECTIONS * quart, blk, hidden), bf16),
            pltpu.VMEM((reps - 1, own_rows, hidden), bf16),
            pltpu.VMEM((reps - 1, own_rows, hidden), bf16),
            pltpu.VMEM((blocks // 2, blk, hidden), bf16),
            pltpu.VMEM((blocks // 2, blk, hidden), bf16),
            pltpu.VMEM((pairs // 2 + SECTIONS * quart, blk, hidden), f32),
            pltpu.VMEM((SECTIONS * quart, blk, hidden), bf16),
            pltpu.VMEM((SECTIONS * quart, blk, hidden), bf16),
            pltpu.VMEM((quart, blk, hidden), bf16),
            pltpu.VMEM((hidden, hidden), f32),
            pltpu.VMEM((2 * share, hidden), f32),
            pltpu.VMEM((2 * share, hidden), f32),
            pltpu.VMEM((share, hidden), f32),
            pltpu.VMEM((levels, share, hidden), f32),
            pltpu.VMEM((levels, share, hidden), f32),
            pltpu.VMEM((hidden, hidden), f32),
            pltpu.VMEM((8, 128), jnp.int32),
            pltpu.SMEM((8, 128), jnp.int32),
            dma((5,)),
            dma((8,)), dma((8,)),
            dma((reps - 1,)), dma((reps - 1,)),
            dma((reps - 1,)), dma((reps - 1,)),
            dma((SECTIONS,)), dma((SECTIONS,)),
            dma((reps - 1,)), dma((reps - 1,)),
            dma((levels,)), dma((levels,)),
            dma((reps - 1,)), dma((reps - 1,)),
        ],
        compiler_params=pltpu.CompilerParams(
            collective_id=0, has_side_effects=True, vmem_limit_bytes=60 * 1024 * 1024
        ),
        cost_estimate=pl.CostEstimate(
            flops=4 * pairs * blk * blk * hidden, bytes_accessed=pairs * blk * blk * 2,
            transcendentals=own_rows * hidden,
        ),
    )(
        block_cols,
        features.reshape(blocks, blk, hidden),
        block_vals.reshape(pairs, blk, blk),
        weight,
        cotangent,
    )
    return pl.pallas_call(
        store_kernel,
        out_shape=tuple(jax.ShapeDtypeStruct(r.shape, r.dtype) for r in results),
        in_specs=[hbm, hbm, hbm],
        out_specs=(hbm, hbm, hbm),
        scratch_shapes=[pltpu.VMEM(r.shape, r.dtype) for r in results] + [dma((3,)), dma((3,))],
        compiler_params=pltpu.CompilerParams(vmem_limit_bytes=60 * 1024 * 1024),
        cost_estimate=pl.CostEstimate(
            flops=0, bytes_accessed=20 * own_rows * hidden, transcendentals=0
        ),
    )(*results)


def solution(mesh):
    return jax.shard_map(
        functools.partial(on_device, mesh.shape["row"], mesh.shape["rep"]),
        mesh=mesh,
        in_specs=(
            P("row", None),
            P("row", "rep", None),
            P("row", "rep", None, None, None),
            P(),
            P(("row", "rep"), None),
        ),
        out_specs=(P(("row", "rep"), None), P(), P(("row", "rep"), None)),
        check_vma=False,
    )
```
